128 devices in a mesh: rows: 4 (over y), cents: 32 (over x, z, core).
Axes of the slice: x: 4, y: 4, z: 4, core: 2. Of those that a mesh axis runs over, the one named last changes fastest.
Arguments:
- vectors: bfloat16 [8192, 1024], P(('rows', 'cents')), may hold values from -24 to 24, as said below
- centroids: bfloat16 [65536, 1024], P('cents'), may hold values from -0.1875 to 0.1875
Outputs:
- updated: bfloat16 [65536, 1024], P('cents', 'rows')
- masses: float32 [65536], P('cents')
The draws below stay inside these ranges and needn't reach their ends.
Inputs may be any that keep to these rules, and one draw needn't show every extreme that they name: `vectors`: entries are real-valued and of order one, with rows of differing scales.
All inputs are finite; a program needn't handle non-finite values.
Results may differ from the reference program's by a relative error of at most 0.015.
Values may be sent and summed in bfloat16 or wider, within the bound.
No kernel may reach another device: no remote copies, remote signals or barrier semaphores. Data moves between devices by JAX's collectives and lax.ppermute only.
A program may use at most 128 MiB of HBM per device.

```python
import math
import jax
import jax.numpy as jnp
from jax import lax

EMBED = 1024
ROUNDS = 3
CENTROIDS = 65536
GROUP_ROWS = 2048
BATCH = 8192
N_ROWS = 4


def draw_vectors(key, part):
    key = jax.random.fold_in(key, 11)
    first_key, second_key = jax.random.split(key)
    rise = 1.0 + 2.0 * jnp.arange(BATCH, dtype=jnp.float32) / max(BATCH - 1, 1)
    spread = jnp.exp(jax.random.uniform(second_key, (BATCH, 1), jnp.float32, math.log(0.5), math.log(2.0)))
    base = jnp.clip(jax.random.normal(first_key, (BATCH, EMBED), jnp.float32), -4.0, 4.0)
    return (base * spread * rise[:, None]).astype(jnp.bfloat16)


def shard_levels(rng, extent, pieces, low, top_value):
    level = 1.0
    for position, parts in pieces:
        draws = jax.random.uniform(jax.random.fold_in(jax.random.fold_in(rng, 6), position), (parts,), jnp.float32, low / len(pieces), top_value / len(pieces))
        level = level * jnp.repeat(jnp.exp(draws), extent[position] // parts).reshape((-1,) + (1,) * (len(extent) - 1 - position))
    return level


def scatter_about(stream_key, shape, width, bound, cuts=(), kind=jnp.bfloat16):
    loudness = shard_levels(stream_key, shape, cuts, -0.22, 0.18) if cuts else 1.0
    result = jax.random.normal(stream_key, shape, jnp.float32) * width * loudness
    return jnp.minimum(jnp.maximum(result, -bound), bound).astype(kind)


def setup_inputs(seed: int = 0) -> dict:
    streams_of = jax.random.split(jax.random.key(seed), 3)
    vectors = draw_vectors(jax.random.fold_in(streams_of[2], 71), 0)
    centroids = scatter_about(streams_of[1], (CENTROIDS, EMBED), EMBED ** -0.5, 0.1875, ((0, 32),))
    return dict(vectors=vectors, centroids=centroids)


SHARP = 0.75


def reference(vectors, centroids):
    logits = jnp.dot(vectors, centroids.T, preferred_element_type=jnp.float32)
    weights = jnp.exp(SHARP * logits)
    target = BATCH / CENTROIDS
    row_scale = jnp.ones((BATCH,), jnp.float32)
    col_scale = jnp.ones((CENTROIDS,), jnp.float32)
    for step in range(ROUNDS):
        colmass = jnp.dot(row_scale, weights, precision=lax.Precision.HIGHEST)
        col_scale = target / colmass
        rowmass = jnp.dot(weights, col_scale, precision=lax.Precision.HIGHEST)
        row_scale = 1.0 / rowmass
    masses = jnp.zeros((CENTROIDS,), jnp.float32)
    sums = jnp.zeros((CENTROIDS, EMBED), jnp.float32)
    for block in range(N_ROWS):
        first = block * GROUP_ROWS
        plan = weights[first:first + GROUP_ROWS] * row_scale[first:first + GROUP_ROWS, None] * col_scale[None, :]
        masses = masses + jnp.sum(plan, axis=0)
        plan_low = plan.astype(jnp.bfloat16)
        partial_value = lax.dot_general(plan_low, vectors[first:first + GROUP_ROWS], (((0,), (0,)), ((), ())), preferred_element_type=jnp.float32)
        partial_value = lax.optimization_barrier(partial_value.astype(jnp.bfloat16))
        sums = sums + partial_value.astype(jnp.float32)
    updated = 0.5 * centroids.astype(jnp.float32) + 0.5 * sums / masses[:, None]
    return updated.astype(jnp.bfloat16), masses
```

```python
import jax
import jax.numpy as jnp
from jax import lax
from jax.experimental import pallas as pl
from jax.experimental.pallas import tpu as pltpu
from jax.sharding import Mesh, PartitionSpec as P

ROUNDS = 3
SHARP = 0.75
LOG2E = 1.4426950408889634
CENTS = ("x", "z", "core")
LANES = 128
TAIL = 32
WEIGH_VMEM = 10 * 1024 * 1024
PLAN_VMEM = 10 * 1024 * 1024
SUM_VMEM = 8 * 1024 * 1024

VM = pl.BlockSpec(memory_space=pltpu.VMEM)
SM = pl.BlockSpec(memory_space=pltpu.SMEM)


def params(vmem):
    return pltpu.CompilerParams(vmem_limit_bytes=vmem)


def held(x):
    return pltpu.with_memory_space_constraint(x, pltpu.VMEM)


def row_of(block):
    return jnp.sum(block.T, axis=0, keepdims=True)


def down(row):
    return jnp.broadcast_to(row, (LANES, LANES)).T


def weigh_kernel(cents_ref, vecs_ref, w_ref, mass_ref, acc_ref):
    n, m = w_ref.shape
    rows, cols = min(n, 512), min(m, 512)
    for k in range(0, n, rows):
        acc = None
        for i in range(0, m, cols):
            logits = lax.dot_general(
                cents_ref[k : k + rows, :],
                vecs_ref[i : i + cols, :],
                (((1,), (1,)), ((), ())),
                preferred_element_type=jnp.float32,
            )
            w = jnp.exp2(logits * (SHARP * LOG2E))
            w_ref[k : k + rows, i : i + cols] = w
            for j in range(0, cols, LANES):
                acc = w[:, j : j + LANES] if acc is None else acc + w[:, j : j + LANES]
        acc_ref[k : k + rows, :] = acc
    for g in range(n // LANES):
        mass_ref[g : g + 1, :] = row_of(acc_ref[g * LANES : (g + 1) * LANES, :])


def weigh(cents, vecs):
    n, d = cents.shape
    m = vecs.shape[0]
    return pl.pallas_call(
        weigh_kernel,
        in_specs=[VM, VM],
        out_specs=[VM, VM],
        out_shape=[pltpu.VMEM((n, m), jnp.float32), jax.ShapeDtypeStruct((n // LANES, LANES), jnp.float32)],
        scratch_shapes=[pltpu.VMEM((n, LANES), jnp.float32)],
        compiler_params=params(WEIGH_VMEM),
        cost_estimate=pl.CostEstimate(flops=2 * n * m * d, bytes_accessed=2 * (n + m) * d, transcendentals=n * m),
        name="weigh",
    )(held(cents), held(vecs))


def row_kernel(target, core_ref, w0_ref, w1_ref, a_ref, b_ref, c_ref, d_ref, out_ref, scale_ref):
    scale_ref[...] = target / ((a_ref[...] + b_ref[...]) + (c_ref[...] + d_ref[...]))
    tiles = w0_ref.shape[1] // LANES
    accs = [None] * (2 * tiles)
    for b in range(w0_ref.shape[0] // LANES):
        part = slice(b * LANES, (b + 1) * LANES)
        s = down(scale_ref[b : b + 1, :])
        for j in range(2 * tiles):
            ref, t = (w0_ref, j) if j < tiles else (w1_ref, j - tiles)
            p = ref[part, t * LANES : (t + 1) * LANES] * s
            p = jnp.sum(p.reshape(LANES // 8, 8, LANES), axis=0)
            accs[j] = p if b == 0 else accs[j] + p
    rows = [jnp.sum(a, axis=0, keepdims=True) for a in accs]
    here = jnp.concatenate(rows[:tiles], axis=0)
    there = jnp.concatenate(rows[tiles:], axis=0)
    first = core_ref[0] == 0
    value = jnp.concatenate([jnp.where(first, here, there), jnp.where(first, there, here)], axis=0)
    for q in range(out_ref.shape[0]):
        out_ref[q] = value


def row_pass(target, core, w, masses, peers):
    n = w[0].shape[0]
    lines = (w[0].shape[1] + w[1].shape[1]) // LANES
    return pl.pallas_call(
        lambda *refs: row_kernel(target, *refs),
        in_specs=[SM] + [VM] * 6,
        out_specs=[VM, VM],
        out_shape=[
            jax.ShapeDtypeStruct((peers, lines, LANES), jnp.float32),
            jax.ShapeDtypeStruct((n // LANES, LANES), jnp.float32),
        ],
        compiler_params=params(8 * 1024 * 1024),
        name="row_pass",
    )(core, held(w[0]), held(w[1]), *masses)


def local_scale(core_ref, sums_ref):
    total = sums_ref[0]
    for q in range(1, sums_ref.shape[0]):
        total = total + sums_ref[q]
    scale = 1.0 / total
    half = scale.shape[0] // 2
    first = core_ref[0] == 0
    a, b = scale[:half], scale[half:]
    return jnp.concatenate([jnp.where(first, a, b), jnp.where(first, b, a)], axis=0)


def col_kernel(core_ref, w0_ref, w1_ref, sums_ref, out_ref):
    scale = local_scale(core_ref, sums_ref)
    tiles = w0_ref.shape[1] // LANES

    for b in range(w0_ref.shape[0] // LANES):
        part = slice(b * LANES, (b + 1) * LANES)
        acc = None
        for j in range(2 * tiles):
            ref, t = (w0_ref, j) if j < tiles else (w1_ref, j - tiles)
            p = ref[part, t * LANES : (t + 1) * LANES] * scale[j : j + 1, :]
            acc = p if acc is None else acc + p
        out_ref[b : b + 1, :] = row_of(acc)


def col_pass(core, w, sums):
    n = w[0].shape[0]
    return pl.pallas_call(
        col_kernel,
        in_specs=[SM] + [VM] * 3,
        out_specs=VM,
        out_shape=jax.ShapeDtypeStruct((n // LANES, LANES), jnp.float32),
        compiler_params=params(8 * 1024 * 1024),
        name="col_pass",
    )(core, held(w[0]), held(w[1]), sums)


def product(plan_ref, v0_ref, v1_ref, rows, cols):
    m = v0_ref.shape[0]
    a = jnp.dot(plan_ref[rows, :m], v0_ref[:, cols], preferred_element_type=jnp.float32)
    return a + jnp.dot(plan_ref[rows, m:], v1_ref[:, cols], preferred_element_type=jnp.float32)


def split(x):
    hi = x.astype(jnp.bfloat16)
    rest = x - hi.astype(jnp.float32)
    mid = rest.astype(jnp.bfloat16)
    return hi, mid, (rest - mid.astype(jnp.float32)).astype(jnp.bfloat16)


def put_tail(ref, x):
    hi, mid, lo = split(x)
    top, lines = ref.shape[0] - TAIL, x.shape[0]
    ref[top : top + lines, :LANES] = hi
    ref[top : top + lines, LANES:] = mid
    ref[top + lines :, :LANES] = lo
    ref[top + lines :, LANES:] = jnp.zeros_like(lo)


def get_tail(ref):
    f32, top, lines = jnp.float32, ref.shape[0] - TAIL, TAIL // 2
    hi, mid = ref[top : top + lines, :LANES].astype(f32), ref[top : top + lines, LANES:].astype(f32)
    return (hi + mid) + ref[top + lines :, :LANES].astype(f32)


def plan_kernel(
    share, place_ref, w0_ref, w1_ref, sums_ref, scale_ref, v0_ref, v1_ref, plan_ref, mass_ref, fa_ref, fb_ref
):
    scale = local_scale(place_ref, sums_ref)
    tiles = w0_ref.shape[1] // LANES
    n = w0_ref.shape[0]
    rows = 2 * LANES
    cols = pl.ds(pl.multiple_of(place_ref[1] * share, share), share)

    def half(first, o_ref):
        def body(b, carry):
            top = first + b * rows
            for g in range(rows // LANES):
                part = pl.ds(pl.multiple_of(top + g * LANES, LANES), LANES)
                line = pl.ds(top // LANES + g, 1)
                s = down(scale_ref[line, :])
                acc = None
                for j in range(2 * tiles):
                    ref, t = (w0_ref, j) if j < tiles else (w1_ref, j - tiles)
                    p = ref[part, t * LANES : (t + 1) * LANES] * scale[j : j + 1, :]
                    acc = p if acc is None else acc + p
                    plan_ref[part, j * LANES : (j + 1) * LANES] = (p * s).astype(jnp.bfloat16)
                mass_ref[line, :] = row_of(acc)
            out = product(plan_ref, v0_ref, v1_ref, pl.ds(pl.multiple_of(top, rows), rows), cols)
            o_ref[pl.ds(pl.multiple_of(b * rows, rows), rows), :] = out.astype(o_ref.dtype)
            return carry

        lax.fori_loop(0, n // 2 // rows, body, 0, unroll=2)

    half(0, fa_ref)
    half(n // 2, fb_ref)
    put_tail(fa_ref, mass_ref[...])
    put_tail(fb_ref, mass_ref[...])


def make_plan(place, w, sums, scale, vecs, share):
    n, m = w[0].shape
    part = jax.ShapeDtypeStruct((n // 2 + TAIL, share), jnp.bfloat16)
    return pl.pallas_call(
        lambda *refs: plan_kernel(share, *refs),
        in_specs=[SM] + [VM] * 6,
        out_specs=[VM] * 4,
        out_shape=[
            pltpu.VMEM((n, 2 * m), jnp.bfloat16),
            jax.ShapeDtypeStruct((n // LANES, LANES), jnp.float32),
            part,
            part,
        ],
        compiler_params=params(PLAN_VMEM),
        name="make_plan",
    )(place, held(w[0]), held(w[1]), sums, scale, held(vecs[0]), held(vecs[1]))


def sum_kernel(first, count, turn, share, planes, place_ref, plan_ref, v0_ref, v1_ref, *refs):
    out_ref = refs[-1]
    rows = 512
    cols = pl.ds(pl.multiple_of(lax.rem(place_ref[1] + turn, planes) * share, share), share)
    for at in range(0, count, rows):
        out = product(plan_ref, v0_ref, v1_ref, slice(first + at, first + at + rows), cols)
        if len(refs) > 1:
            out = out + refs[0][at : at + rows, :].astype(jnp.float32)
        out_ref[at : at + rows, :] = out.astype(out_ref.dtype)
    if len(refs) > 1:
        out_ref[count:, :] = refs[0][count:, :]


def slice_sum(place, plan, vecs, planes, turn, first, count, dtype, arrived=None):
    more = [] if arrived is None else [arrived]
    m, d = vecs[0].shape
    share = d // planes
    return pl.pallas_call(
        lambda *refs: sum_kernel(first, count, turn, share, planes, *refs),
        in_specs=[SM] + [VM] * (3 + len(more)),
        out_specs=VM,
        out_shape=jax.ShapeDtypeStruct((count + (TAIL if more else 0), share), dtype),
        compiler_params=params(SUM_VMEM),
        cost_estimate=pl.CostEstimate(
            flops=4 * count * m * share, bytes_accessed=4 * (count + m) * share, transcendentals=0
        ),
        name="slice_sum",
    )(place, held(plan), held(vecs[0]), held(vecs[1]), *more)


def finish_kernel(share, place_ref, cents_ref, own_ref, scale_ref, m_ref, fa, fb, ua, ub, da, db, out_ref, mass_ref):
    mass_ref[...] = scale_ref[...] * ((m_ref[...] + get_tail(ua)) + (get_tail(fa) + get_tail(fb)))
    n = out_ref.shape[0]
    half = n // 2
    f32 = jnp.float32
    for line in range(n // LANES):
        part = slice(line * LANES, (line + 1) * LANES)
        up, dn, at = (ua, da, 0) if line * LANES < half else (ub, db, half)
        there = slice(part.start - at, part.stop - at)
        sums = own_ref[part, :] + (up[there, :].astype(f32) + dn[there, :].astype(f32))
        inverse = down(0.5 / mass_ref[line : line + 1, :])
        for j in range(0, share, LANES):
            value = 0.5 * cents_ref[part, j : j + LANES].astype(f32) + sums[:, j : j + LANES] * inverse
            out_ref[part, j : j + LANES] = value.astype(out_ref.dtype)


def finish(place, centroids, own, scale, mass, arrived):
    n, share = own.shape
    return pl.pallas_call(
        lambda *refs: finish_kernel(share, *refs),
        grid_spec=pltpu.PrefetchScalarGridSpec(
            num_scalar_prefetch=1,
            grid=(1,),
            in_specs=[pl.BlockSpec((n, share), lambda i, place: (0, place[2]))] + [VM] * 9,
            out_specs=[VM, VM],
        ),
        out_shape=[
            jax.ShapeDtypeStruct((n, share), jnp.bfloat16),
            jax.ShapeDtypeStruct(scale.shape, jnp.float32),
        ],
        compiler_params=params(16 * 1024 * 1024),
        name="finish",
    )(place, centroids, own, scale, mass, *arrived)


def move(x, axis, by):
    n = lax.axis_size(axis)
    return lax.ppermute(x, axis, [(i, (i + by) % n) for i in range(n)])


def row_peers(x):
    return x, move(x, "y", 2), move(x, "y", 1), move(x, "y", 3)


def body(vectors, centroids):
    planes = lax.axis_size("y")
    core, y = lax.axis_index("core"), lax.axis_index("y")
    place = jnp.stack([core, lax.rem(y + 2, planes), y]).astype(jnp.int32)
    side = lax.axis_size("x") * lax.axis_size("z")
    peers = side * lax.axis_size("core")
    n, d = centroids.shape
    share = d // planes
    target = vectors.shape[0] * planes * peers / (n * peers)

    copies = jnp.broadcast_to(vectors[None], (side,) + vectors.shape)
    mine = lax.all_to_all(copies, ("x", "z"), 0, 0, tiled=True).reshape(side * vectors.shape[0], d)
    other = move(mine, "core", 1)
    vecs = (mine, other)
    w0, mass0 = weigh(centroids, mine)
    w1, mass1 = weigh(centroids, other)
    w = (w0, w1)

    colmass = mass0 + mass1
    for step in range(ROUNDS):
        sums, scale = row_pass(target, place, w, row_peers(colmass), peers)
        sums = lax.all_to_all(sums, CENTS, 0, 0, tiled=True)
        if step < ROUNDS - 1:
            colmass = col_pass(place, w, sums)

    half = n // 2
    low = jnp.bfloat16

    def part(turn, first, count, dtype, arrived=None):
        return slice_sum(place, plan, vecs, planes, turn, first, count, dtype, arrived)

    plan, colmass, far_a, far_b = make_plan(place, w, sums, scale, vecs, share)
    far_a, far_b = move(far_a, "y", 1), move(far_b, "y", 3)
    up_b = move(part(3, half, half, low), "y", 1)
    down_a = move(part(1, 0, half, low), "y", 3)
    own = part(2, 0, n, jnp.float32)
    own, far_a, far_b = lax.optimization_barrier((own, far_a, far_b))
    up_a = move(part(3, 0, half, low, far_a), "y", 1)
    down_b = move(part(1, half, half, low, far_b), "y", 3)
    updated, masses = finish(place, centroids, own, scale, colmass, (far_a, far_b, up_a, up_b, down_a, down_b))
    return updated, masses.reshape(n)


def solution(mesh):
    sizes = (mesh.shape["rows"], 4, 4, 2)
    torus = Mesh(mesh.devices.reshape(sizes), ("y",) + CENTS)
    return jax.shard_map(
        body,
        mesh=torus,
        in_specs=(P(("y",) + CENTS, None), P(CENTS, None)),
        out_specs=(P(CENTS, "y"), P(CENTS)),
        check_vma=False,
    )
```

```python
import functools

import jax
import jax.numpy as jnp
from jax import lax
from jax.experimental import pallas as pl
from jax.experimental.pallas import tpu as pltpu
from jax.sharding import Mesh, PartitionSpec as P

ROUNDS = 3
SHARP = 0.75
LOG2E = 1.4426950408889634
CENTS = ("x", "z", "core")
LANES = 128
TAIL = 16
PLACES = 4
LINES = 2
ORDER = ((True, 0), (False, 0), (True, 1), (True, 2), (True, 3), (False, 1), (False, 2), (False, 3))
FLOPS = 3 * 10**10
WEIGH_VMEM = 16 * 1024 * 1024
SUM_VMEM = 10 * 1024 * 1024

VM = pl.BlockSpec(memory_space=pltpu.VMEM)
SM = pl.BlockSpec(memory_space=pltpu.SMEM)


def params(vmem):
    return pltpu.CompilerParams(vmem_limit_bytes=vmem)


def held(x):
    return pltpu.with_memory_space_constraint(x, pltpu.VMEM)


def outside(x):
    return pltpu.with_memory_space_constraint(x, pltpu.HBM)


def row_of(block):
    return jnp.sum(block.T, axis=0, keepdims=True)


def down(row):
    return jnp.broadcast_to(row, (LANES, LANES)).T


def line_of(place_ref, mine, turn):
    core = place_ref[0]
    place, side = (place_ref[2], core) if mine else (place_ref[3], 1 - core)
    return pl.multiple_of((side * PLACES + lax.rem(place + PLACES - turn, PLACES)) * LINES, LINES)


def gather_kernel(place_ref, *refs):
    blocks, out = refs[:-1], refs[-1]
    size = blocks[0].shape[0]
    for turn, block in enumerate(blocks):
        at = lax.rem(place_ref[4] + PLACES - turn, PLACES) * size
        out[pl.ds(pl.multiple_of(at, size), size), :] = block[...]


def in_order(place, blocks):
    size, d = blocks[0].shape
    return pl.pallas_call(
        gather_kernel,
        in_specs=[SM] + [VM] * len(blocks),
        out_specs=VM,
        out_shape=jax.ShapeDtypeStruct((len(blocks) * size, d), blocks[0].dtype),
        compiler_params=params(8 * 1024 * 1024),
        name="in_order",
    )(place, *blocks)


def weigh_kernel(count, cuts, place_ref, cents_ref, *refs):
    blocks, every = refs[:count], refs[count : count + cuts * 2]
    w_ref, mass_ref, *outs = refs[count + cuts * 2 : count + cuts * 3 + 2]
    acc_ref, sem = refs[-2:]
    n = w_ref.shape[0]
    rows = 512
    copies = []
    for k, out in enumerate(outs):
        share = out.shape[1]
        part = pl.ds(pl.multiple_of(lax.rem(place_ref[1] + k, cuts) * share, share), share)
        for i, block in enumerate(every):
            size = block.shape[0]
            copies.append(
                pltpu.make_async_copy(block.at[:, part], out.at[pl.ds(i * size, size)], sem.at[len(copies)])
            )
    for copy in copies:
        copy.start()
    for k in range(0, n, rows):
        acc, at = None, 0
        for block in blocks:
            cols = block.shape[0]
            logits = lax.dot_general(
                cents_ref[k : k + rows, :], block[...], (((1,), (1,)), ((), ())), preferred_element_type=jnp.float32
            )
            w = jnp.exp2(logits * (SHARP * LOG2E))
            w_ref[k : k + rows, at : at + cols] = w
            at += cols
            for j in range(0, cols, LANES):
                acc = w[:, j : j + LANES] if acc is None else acc + w[:, j : j + LANES]
        acc_ref[k : k + rows, :] = acc
    for g in range(n // LANES):
        mass_ref[g : g + 1, :] = row_of(acc_ref[g * LANES : (g + 1) * LANES, :])
    for copy in copies:
        copy.wait()


def weigh(place, cents, blocks, cuts=0, every=()):
    n, d = cents.shape
    m = sum(block.shape[0] for block in blocks)
    total = sum(block.shape[0] for block in every)
    return pl.pallas_call(
        functools.partial(weigh_kernel, len(blocks), cuts),
        in_specs=[SM, VM] + [VM] * len(blocks) + [pl.BlockSpec(memory_space=pl.ANY)] * len(every),
        out_specs=[VM] * (2 + cuts),
        out_shape=[pltpu.VMEM((n, m), jnp.float32), jax.ShapeDtypeStruct((n // LANES, LANES), jnp.float32)]
        + [pltpu.VMEM((total, d // cuts), cents.dtype) for _ in range(cuts)],
        scratch_shapes=[
            pltpu.VMEM((n, LANES), jnp.float32),
            pltpu.SemaphoreType.DMA((max(len(every) * cuts, 1),)),
        ],
        compiler_params=params(WEIGH_VMEM),
        cost_estimate=pl.CostEstimate(flops=FLOPS, bytes_accessed=0, transcendentals=0),
        name="weigh",
    )(place, held(cents), *[held(block) for block in blocks], *every)


def tiles_of(w_refs):
    return [(ref, t) for ref in w_refs for t in range(0, ref.shape[1], LANES)]


def row_kernel(target, place_ref, w0_ref, w1_ref, w2_ref, a_ref, b_ref, c_ref, d_ref, out_ref, scale_ref, lines_ref):
    scale_ref[...] = target / ((a_ref[...] + b_ref[...]) + (c_ref[...] + d_ref[...]))
    tiles = tiles_of((w0_ref, w1_ref, w2_ref))
    accs = [None] * len(tiles)
    for b in range(w0_ref.shape[0] // LANES):
        part = slice(b * LANES, (b + 1) * LANES)
        s = down(scale_ref[b : b + 1, :])
        for j, (ref, t) in enumerate(tiles):
            p = ref[part, t : t + LANES] * s
            p = jnp.sum(p.reshape(LANES // 8, 8, LANES), axis=0)
            accs[j] = p if b == 0 else accs[j] + p
    for block, (mine, turn) in enumerate(ORDER):
        pair = [jnp.sum(a, axis=0, keepdims=True) for a in accs[block * LINES : (block + 1) * LINES]]
        lines_ref[pl.ds(line_of(place_ref, mine, turn), LINES), :] = jnp.concatenate(pair, axis=0)
    value = lines_ref[...].astype(out_ref.dtype)
    for q in range(out_ref.shape[0]):
        out_ref[q] = value


def row_pass(target, place, w, masses, peers):
    n = w[0].shape[0]
    lines = len(ORDER) * LINES
    return pl.pallas_call(
        lambda *refs: row_kernel(target, *refs),
        in_specs=[SM] + [VM] * 7,
        out_specs=[VM, VM],
        out_shape=[
            jax.ShapeDtypeStruct((peers, lines, LANES), jnp.bfloat16),
            jax.ShapeDtypeStruct((n // LANES, LANES), jnp.float32),
        ],
        scratch_shapes=[pltpu.VMEM((lines, LANES), jnp.float32)],
        compiler_params=params(8 * 1024 * 1024),
        name="row_pass",
    )(place, *[held(x) for x in w], *masses)


def local_scale(place_ref, sums_ref, lines_ref):
    total = sums_ref[0].astype(jnp.float32)
    for q in range(1, sums_ref.shape[0]):
        total = total + sums_ref[q].astype(jnp.float32)
    lines_ref[...] = 1.0 / total
    scale = [lines_ref[pl.ds(line_of(place_ref, mine, turn), LINES), :] for mine, turn in ORDER]
    return [pair[i : i + 1, :] for pair in scale for i in range(LINES)]


def col_kernel(place_ref, w0_ref, w1_ref, w2_ref, sums_ref, out_ref, lines_ref):
    scale = local_scale(place_ref, sums_ref, lines_ref)
    tiles = tiles_of((w0_ref, w1_ref, w2_ref))
    for b in range(w0_ref.shape[0] // LANES):
        part = slice(b * LANES, (b + 1) * LANES)
        acc = None
        for j, (ref, t) in enumerate(tiles):
            p = ref[part, t : t + LANES] * scale[j]
            acc = p if acc is None else acc + p
        out_ref[b : b + 1, :] = row_of(acc)


def col_pass(place, w, sums):
    n = w[0].shape[0]
    return pl.pallas_call(
        col_kernel,
        in_specs=[SM] + [VM] * 4,
        out_specs=VM,
        out_shape=jax.ShapeDtypeStruct((n // LANES, LANES), jnp.float32),
        scratch_shapes=[pltpu.VMEM(sums.shape[1:], jnp.float32)],
        compiler_params=params(8 * 1024 * 1024),
        name="col_pass",
    )(place, *[held(x) for x in w], sums)


def split(x):
    hi = x.astype(jnp.bfloat16)
    rest = x - hi.astype(jnp.float32)
    mid = rest.astype(jnp.bfloat16)
    return hi, mid, (rest - mid.astype(jnp.float32)).astype(jnp.bfloat16)


def put_tail(ref, x):
    hi, mid, lo = split(x)
    tail = slice(ref.shape[0] - TAIL, ref.shape[0])
    ref[tail, :LANES] = jnp.concatenate([hi, mid], axis=0)
    ref[tail, LANES:] = jnp.concatenate([lo, jnp.zeros_like(lo)], axis=0)


def get_tail(ref):
    f32 = jnp.float32
    tail = slice(ref.shape[0] - TAIL, ref.shape[0])
    first, second = ref[tail, :LANES].astype(f32), ref[tail, LANES:].astype(f32)
    return (first[: TAIL // 2] + first[TAIL // 2 :]) + second[: TAIL // 2]


def product(plan, v_ref):
    return jnp.dot(plan, v_ref[...], preferred_element_type=jnp.float32)


def call(kernel, name, specs, out_shape, args, scratch=()):
    return pl.pallas_call(
        kernel,
        in_specs=specs,
        out_specs=[VM] * len(out_shape),
        out_shape=out_shape,
        scratch_shapes=list(scratch),
        compiler_params=params(SUM_VMEM),
        cost_estimate=pl.CostEstimate(flops=FLOPS, bytes_accessed=0, transcendentals=0),
        name=name,
    )(*args)


def plan_kernel(
    first, place_ref, w0_ref, w1_ref, w2_ref, sums_ref, scale_ref, mark_ref, u_ref, f_ref, d_ref, *refs
):
    plan_ref, mass_ref, up_ref, down_ref, lines_ref = refs
    scale = local_scale(place_ref, sums_ref, lines_ref)
    tiles = tiles_of((w0_ref, w1_ref, w2_ref))
    rows = 2 * LANES
    n = plan_ref.shape[0]
    half = n // 2
    for top in range(0, n, rows):
        for at in range(top, top + rows, LANES):
            part = slice(first + at, first + at + LANES)
            line = (first + at) // LANES
            s = down(scale_ref[line : line + 1, :])
            acc = None
            for j, (ref, t) in enumerate(tiles):
                p = ref[part, t : t + LANES] * scale[j]
                acc = p if acc is None else acc + p
                plan_ref[at : at + LANES, j * LANES : (j + 1) * LANES] = (p * s).astype(jnp.bfloat16)
            mass_ref[at // LANES : at // LANES + 1, :] = row_of(acc)
        here = plan_ref[top : top + rows, :]
        far, near, at, v_ref = (up_ref, down_ref, top, d_ref) if top < half else (down_ref, up_ref, top - half, u_ref)
        far[at : at + rows, :] = product(here, f_ref).astype(far.dtype)
        near[half + at : half + at + rows, :] = product(here, v_ref).astype(near.dtype)
    put_tail(up_ref, mass_ref[...])
    put_tail(down_ref, mass_ref[...])


def make_plan(place, w, sums, scale, cuts, first, mark):
    n = w[0].shape[0]
    m, share = cuts[0].shape
    part = jax.ShapeDtypeStruct((n // 2 + TAIL, share), jnp.bfloat16)
    return call(
        lambda *refs: plan_kernel(first, *refs),
        "make_plan",
        [SM] + [VM] * 9,
        [pltpu.VMEM((n // 2, m), jnp.bfloat16), jax.ShapeDtypeStruct((n // 2 // LANES, LANES), jnp.float32), part, part],
        (place, *[held(x) for x in w], sums, scale, mark, *[held(v) for v in cuts[1:]]),
        [pltpu.VMEM(sums.shape[1:], jnp.float32)],
    )


def late_kernel(plan_ref, from_below, from_above, u_ref, d_ref, up_ref, down_ref, mark_ref):
    half = plan_ref.shape[0] // 2
    f32 = jnp.float32
    up = product(plan_ref[:half, :], u_ref) + from_below[:half, :].astype(f32)
    up_ref[:half, :] = up.astype(up_ref.dtype)
    below = product(plan_ref[half:, :], d_ref) + from_above[:half, :].astype(f32)
    down_ref[:half, :] = below.astype(down_ref.dtype)
    up_ref[half:, :] = from_below[2 * half :, :]
    down_ref[half:, :] = from_above[2 * half :, :]
    mark_ref[...] = jnp.zeros_like(mark_ref)


def late_sums(plan, from_below, from_above, cuts):
    n = plan.shape[0]
    share = cuts[0].shape[1]
    out = jax.ShapeDtypeStruct((n // 2 + TAIL, share), jnp.bfloat16)
    mark = jax.ShapeDtypeStruct((8, LANES), jnp.float32)
    return call(
        late_kernel,
        "late_sums",
        [VM] * 5,
        [out, out, mark],
        (held(plan), from_below, from_above, held(cuts[1]), held(cuts[3])),
    )


def own_kernel(index, place_ref, plan_ref, from_below, from_above, v_ref, mark_ref, cents_ref, out_ref, block_ref, sem):
    n, share = out_ref.shape
    half = n // 2
    f32 = jnp.float32
    cols = pl.ds(pl.multiple_of(place_ref[1] * share, share), share)
    copy = pltpu.make_async_copy(cents_ref.at[pl.ds(index * n, n), cols], block_ref, sem)
    copy.start()
    out_ref[:half, :] = product(plan_ref[:half, :], v_ref) + from_above[half : 2 * half, :].astype(f32)
    out_ref[half:, :] = product(plan_ref[half:, :], v_ref) + from_below[half : 2 * half, :].astype(f32)
    copy.wait()


def own_sums(place, plan, from_below, from_above, cuts, mark, centroids, index):
    n, share = plan.shape[0], cuts[0].shape[1]
    return call(
        functools.partial(own_kernel, index),
        "own_sums",
        [SM] + [VM] * 5 + [pl.BlockSpec(memory_space=pltpu.HBM)],
        [pltpu.VMEM((n, share), jnp.float32), pltpu.VMEM((n, share), centroids.dtype)],
        (place, held(plan), from_below, from_above, held(cuts[0]), mark, outside(centroids)),
        [pltpu.SemaphoreType.DMA],
    )


def finish_kernel(index, place_ref, own_ref, scale_ref, m_ref, below, above, up_ref, down_ref, mark_ref, cents_ref, out_ref, mass_ref):
    lines = mass_ref.shape[0]
    scale = scale_ref[index * lines : (index + 1) * lines, :]
    mass_ref[...] = scale * ((m_ref[...] + get_tail(up_ref)) + (get_tail(below) + get_tail(above)))
    n, share = out_ref.shape
    half = n // 2
    f32 = jnp.float32
    for top in range(0, n, LANES):
        part = slice(top, top + LANES)
        line = top // LANES
        late, start = (up_ref, top) if top < half else (down_ref, top - half)
        sums = own_ref[part, :] + late[start : start + LANES, :].astype(f32)
        inverse = down(0.5 / mass_ref[line : line + 1, :])
        for j in range(0, share, LANES):
            value = 0.5 * cents_ref[part, j : j + LANES].astype(f32) + sums[:, j : j + LANES] * inverse
            out_ref[part, j : j + LANES] = value.astype(out_ref.dtype)


def finish(place, own, scale, mass, below, above, up, under, mark, index, whole=None):
    own, block = own
    n, share = own.shape
    lines = n // LANES
    specs = [VM] * 9
    args = [held(own), scale, mass, below, above, up, under, mark, held(block)]
    kernel = functools.partial(finish_kernel, index)
    if whole is not None:
        specs.append(pl.BlockSpec(memory_space=pl.ANY))
        args.append(whole)

        def kernel(*refs):
            finish_kernel(index, *refs[:10], *refs[11:])

    return pl.pallas_call(
        kernel,
        grid_spec=pltpu.PrefetchScalarGridSpec(
            num_scalar_prefetch=1,
            grid=(1,),
            in_specs=specs,
            out_specs=[pl.BlockSpec((n, share), lambda i, place: (index, 0)), VM],
        ),
        out_shape=[
            jax.ShapeDtypeStruct((2 * n, share), jnp.bfloat16),
            jax.ShapeDtypeStruct((lines, LANES), jnp.float32),
        ],
        input_output_aliases={} if whole is None else {10: 0},
        compiler_params=params(SUM_VMEM),
        cost_estimate=pl.CostEstimate(flops=FLOPS, bytes_accessed=0, transcendentals=0),
        name="finish",
    )(place, *args)


def move(x, axis, by):
    n = lax.axis_size(axis)
    return lax.ppermute(x, axis, [(i, (i + by) % n) for i in range(n)])


def spread(x, turn, first):
    if turn == 0:
        return x
    pairs = []
    for i in range(PLACES):
        for j in range(PLACES):
            for core in range(2):
                by_x = (core == 0) == first
                to = ((i + turn) % PLACES, j) if by_x else (i, (j + turn) % PLACES)
                pairs.append(((i * PLACES + j) * 2 + core, (to[0] * PLACES + to[1]) * 2 + core))
    return lax.ppermute(x, CENTS, pairs)


def row_peers(x):
    return x, move(x, "y", 2), move(x, "y", 1), move(x, "y", 3)


def body(vectors, centroids):
    planes = lax.axis_size("y")
    core, x, z, y = [lax.axis_index(name) for name in ("core", "x", "z", "y")]
    first = core == 0
    place = jnp.stack([core, y, jnp.where(first, z, x), jnp.where(first, x, z), jnp.where(first, x, z)])
    place = place.astype(jnp.int32)
    peers = PLACES * PLACES * lax.axis_size("core")
    n, d = centroids.shape
    target = vectors.shape[0] * planes * peers / (n * peers)

    near = in_order(place, [spread(vectors, turn, True) for turn in range(PLACES)])
    mine = [spread(near, turn, False) for turn in range(PLACES)]
    other = [move(mine[0], "core", 1)]
    w0, mass0 = weigh(place, centroids, (mine[0], other[0]))
    mass0, *mine[1:] = lax.optimization_barrier((mass0, *mine[1:]))
    other += [move(block, "core", 1) for block in mine[1:]]
    every = (mine[0], other[0], *mine[1:], *other[1:])
    w1, mass1 = weigh(place, centroids, mine[1:])
    w2, mass2, *cuts = weigh(place, centroids, other[1:], planes, every)
    w = (w0, w1, w2)

    colmass = mass0 + mass1 + mass2
    for step in range(ROUNDS):
        sums, scale = row_pass(target, place, w, row_peers(colmass), peers)
        sums = lax.all_to_all(sums, CENTS, 0, 0, tiled=True)
        if step < ROUNDS - 1:
            colmass = col_pass(place, w, sums)

    mark = jnp.zeros((8, LANES), jnp.float32)
    plan0, mass0, up0, down0 = make_plan(place, w, sums, scale, cuts, 0, mark)
    up0, down0 = move(up0, "y", 1), move(down0, "y", 3)
    plan1, mass1, up1, down1 = make_plan(place, w, sums, scale, cuts, n // 2, mass0)
    up1, down1 = move(up1, "y", 1), move(down1, "y", 3)
    late_up0, late_down0, mark0 = late_sums(plan0, up0, down0, cuts)
    late_up0, late_down0 = move(late_up0, "y", 1), move(late_down0, "y", 3)
    own0 = own_sums(place, plan0, up0, down0, cuts, mark0, centroids, 0)
    late_up1, late_down1, mark1 = late_sums(plan1, up1, down1, cuts)
    late_up1, late_down1 = move(late_up1, "y", 1), move(late_down1, "y", 3)
    own1 = own_sums(place, plan1, up1, down1, cuts, mark1, centroids, 1)
    half, masses0 = finish(place, own0, scale, mass0, up0, down0, late_up0, late_down0, mark1, 0)
    updated, masses1 = finish(
        place, own1, scale, mass1, up1, down1, late_up1, late_down1, mark1, 1, half
    )
    masses = jnp.concatenate([masses0, masses1], axis=0)
    return updated, masses.reshape(n)


def solution(mesh):
    sizes = (mesh.shape["rows"], 4, 4, 2)
    torus = Mesh(mesh.devices.reshape(sizes), ("y",) + CENTS)
    return jax.shard_map(
        body,
        mesh=torus,
        in_specs=(P(("y",) + CENTS, None), P(CENTS, None)),
        out_specs=(P(CENTS, "y"), P(CENTS)),
        check_vma=False,
    )
```

```python
import functools

import jax
import jax.numpy as jnp
from jax import lax
from jax.experimental import pallas as pl
from jax.experimental.pallas import tpu as pltpu
from jax.sharding import Mesh, PartitionSpec as P

ROUNDS = 3
SHARP = 0.75
LOG2E = 1.4426950408889634
CENTS = ("x", "z", "core")
LANES = 128
TAIL = 16
PLACES = 4
PLANES = 4
LINES = 2
ORDER = ((True, 0), (False, 0), (True, 1), (True, 3), (False, 1), (False, 3), (True, 2), (False, 2))
PARTS = 3
FLOPS = 3 * 10**10
WEIGH_VMEM = 16 * 1024 * 1024
SUM_VMEM = 10 * 1024 * 1024

VM = pl.BlockSpec(memory_space=pltpu.VMEM)
SM = pl.BlockSpec(memory_space=pltpu.SMEM)


def params(vmem):
    return pltpu.CompilerParams(vmem_limit_bytes=vmem)


def held(x):
    return pltpu.with_memory_space_constraint(x, pltpu.VMEM)


def outside(x):
    return pltpu.with_memory_space_constraint(x, pltpu.HBM)


def row_of(block):
    return jnp.sum(block.T, axis=0, keepdims=True)


def down(row):
    return jnp.broadcast_to(row, (LANES, LANES)).T


def line_of(place_ref, mine, turn):
    core = place_ref[0]
    place, side = (place_ref[2], core) if mine else (place_ref[3], 1 - core)
    return pl.multiple_of((side * PLACES + lax.rem(place + PLACES - turn, PLACES)) * LINES, LINES)


def gather_kernel(place_ref, *refs):
    blocks, out = refs[:-1], refs[-1]
    size = blocks[0].shape[0]
    for turn, block in enumerate(blocks):
        at = lax.rem(place_ref[4] + PLACES - turn, PLACES) * size
        out[pl.ds(pl.multiple_of(at, size), size), :] = block[...]


def in_order(place, blocks):
    size, d = blocks[0].shape
    return pl.pallas_call(
        gather_kernel,
        in_specs=[SM] + [VM] * len(blocks),
        out_specs=VM,
        out_shape=jax.ShapeDtypeStruct((len(blocks) * size, d), blocks[0].dtype),
        compiler_params=params(8 * 1024 * 1024),
        name="in_order",
    )(place, *blocks)


def weigh_kernel(count, at, last, place_ref, cents_ref, *refs):
    blocks = refs[:count]
    olds = 0 if at == 0 else PLANES + 1
    w_ref, *outs = refs[count + olds :]
    cuts, acc_ref = (outs[:-2], outs[-2]) if last else (outs[:-1], outs[-1])
    n = w_ref.shape[0]
    rows = 512
    full = LANES * LINES
    groups = []
    for block in blocks:
        if groups and sum(x.shape[0] for x in groups[-1]) < full:
            groups[-1].append(block)
        else:
            groups.append([block])
    for k in range(0, n, rows):
        acc, left = None if at == 0 else acc_ref[k : k + rows, :], 0
        for group in groups:
            vecs = jnp.concatenate([block[...] for block in group], axis=0)
            cols = vecs.shape[0]
            logits = lax.dot_general(
                cents_ref[k : k + rows, :], vecs, (((1,), (1,)), ((), ())), preferred_element_type=jnp.float32
            )
            w = jnp.exp2(logits * (SHARP * LOG2E))
            w_ref[k : k + rows, left : left + cols] = w
            left += cols
            for j in range(0, cols, LANES):
                acc = w[:, j : j + LANES] if acc is None else acc + w[:, j : j + LANES]
        if not last:
            acc_ref[k : k + rows, :] = acc
        else:
            for g in range(0, rows, LANES):
                line = (k + g) // LANES
                outs[-1][line : line + 1, :] = row_of(acc[g : g + LANES, :])
    for k, cut in enumerate(cuts):
        share, top = cut.shape[1], at
        part = pl.ds(pl.multiple_of(lax.rem(place_ref[1] + k, len(cuts)) * share, share), share)
        for block in blocks:
            cut[top : top + block.shape[0], :] = block[:, part]
            top += block.shape[0]


def weigh(place, cents, blocks, planes, total, at, old=()):
    n, d = cents.shape
    m = sum(block.shape[0] for block in blocks)
    last = at + m == total
    out_shape = [pltpu.VMEM((n, m), jnp.float32)]
    out_shape += [pltpu.VMEM((total, d // planes), cents.dtype) for _ in range(planes)]
    out_shape += [pltpu.VMEM((n, LANES), jnp.float32)]
    if last:
        out_shape += [jax.ShapeDtypeStruct((n // LANES, LANES), jnp.float32)]
    return pl.pallas_call(
        functools.partial(weigh_kernel, len(blocks), at, last),
        in_specs=[SM] + [VM] * (1 + len(blocks) + len(old)),
        out_specs=[VM] * len(out_shape),
        out_shape=out_shape,
        input_output_aliases={2 + len(blocks) + k: 1 + k for k in range(len(old))},
        compiler_params=params(WEIGH_VMEM),
        cost_estimate=pl.CostEstimate(flops=FLOPS, bytes_accessed=0, transcendentals=0),
        name="weigh",
    )(place, held(cents), *[held(x) for x in (*blocks, *old)])


def lift_kernel(x_ref, out_ref):
    out_ref[...] = x_ref[...]


def lift(x):
    return pl.pallas_call(
        lift_kernel,
        in_specs=[VM],
        out_specs=VM,
        out_shape=pltpu.VMEM(x.shape, x.dtype),
        compiler_params=params(8 * 1024 * 1024),
        cost_estimate=pl.CostEstimate(flops=FLOPS, bytes_accessed=0, transcendentals=0),
        name="lift",
    )(outside(x))


def tiles_of(w_refs):
    return [(ref, t) for ref in w_refs for t in range(0, ref.shape[1], LANES)]


def row_kernel(target, place_ref, *refs):
    w_refs, (a_ref, b_ref, c_ref, d_ref, out_ref, scale_ref, lines_ref) = refs[:PARTS], refs[PARTS:]
    scale_ref[...] = target / ((a_ref[...] + b_ref[...]) + (c_ref[...] + d_ref[...]))
    tiles = tiles_of(w_refs)
    accs = [None] * len(tiles)
    for b in range(w_refs[0].shape[0] // LANES):
        part = slice(b * LANES, (b + 1) * LANES)
        s = down(scale_ref[b : b + 1, :])
        for j, (ref, t) in enumerate(tiles):
            p = ref[part, t : t + LANES] * s
            p = jnp.sum(p.reshape(LANES // 8, 8, LANES), axis=0)
            accs[j] = p if b == 0 else accs[j] + p
    for block, (mine, turn) in enumerate(ORDER):
        pair = [jnp.sum(a, axis=0, keepdims=True) for a in accs[block * LINES : (block + 1) * LINES]]
        lines_ref[pl.ds(line_of(place_ref, mine, turn), LINES), :] = jnp.concatenate(pair, axis=0)
    value = lines_ref[...].astype(out_ref.dtype)
    for q in range(out_ref.shape[0]):
        out_ref[q] = value


def row_pass(target, place, w, masses, peers):
    n = w[0].shape[0]
    lines = len(ORDER) * LINES
    return pl.pallas_call(
        lambda *refs: row_kernel(target, *refs),
        in_specs=[SM] + [VM] * (PARTS + 4),
        out_specs=[VM, VM],
        out_shape=[
            jax.ShapeDtypeStruct((peers, lines, LANES), jnp.bfloat16),
            jax.ShapeDtypeStruct((n // LANES, LANES), jnp.float32),
        ],
        scratch_shapes=[pltpu.VMEM((lines, LANES), jnp.float32)],
        compiler_params=params(8 * 1024 * 1024),
        name="row_pass",
    )(place, *[held(x) for x in w], *masses)


def local_scale(place_ref, sums_ref, lines_ref):
    total = sums_ref[0].astype(jnp.float32)
    for q in range(1, sums_ref.shape[0]):
        total = total + sums_ref[q].astype(jnp.float32)
    lines_ref[...] = 1.0 / total
    scale = [lines_ref[pl.ds(line_of(place_ref, mine, turn), LINES), :] for mine, turn in ORDER]
    return [pair[i : i + 1, :] for pair in scale for i in range(LINES)]


def col_kernel(place_ref, *refs):
    w_refs, (sums_ref, out_ref, lines_ref) = refs[:PARTS], refs[PARTS:]
    scale = local_scale(place_ref, sums_ref, lines_ref)
    tiles = tiles_of(w_refs)
    for b in range(w_refs[0].shape[0] // LANES):
        part = slice(b * LANES, (b + 1) * LANES)
        acc = None
        for j, (ref, t) in enumerate(tiles):
            p = ref[part, t : t + LANES] * scale[j]
            acc = p if acc is None else acc + p
        out_ref[b : b + 1, :] = row_of(acc)


def col_pass(place, w, sums):
    n = w[0].shape[0]
    return pl.pallas_call(
        col_kernel,
        in_specs=[SM] + [VM] * (PARTS + 1),
        out_specs=VM,
        out_shape=jax.ShapeDtypeStruct((n // LANES, LANES), jnp.float32),
        scratch_shapes=[pltpu.VMEM(sums.shape[1:], jnp.float32)],
        compiler_params=params(8 * 1024 * 1024),
        name="col_pass",
    )(place, *[held(x) for x in w], sums)


def split(x):
    hi = x.astype(jnp.bfloat16)
    rest = x - hi.astype(jnp.float32)
    mid = rest.astype(jnp.bfloat16)
    return hi, mid, (rest - mid.astype(jnp.float32)).astype(jnp.bfloat16)


def put_tail(ref, x):
    hi, mid, lo = split(x)
    tail = slice(ref.shape[0] - TAIL, ref.shape[0])
    ref[tail, :LANES] = jnp.concatenate([hi, mid], axis=0)
    ref[tail, LANES:] = jnp.concatenate([lo, jnp.zeros_like(lo)], axis=0)


def get_tail(ref):
    f32 = jnp.float32
    tail = slice(ref.shape[0] - TAIL, ref.shape[0])
    first, second = ref[tail, :LANES].astype(f32), ref[tail, LANES:].astype(f32)
    return (first[: TAIL // 2] + first[TAIL // 2 :]) + second[: TAIL // 2]


def product(plan, v_ref):
    return jnp.dot(plan, v_ref[...], preferred_element_type=jnp.float32)


def call(kernel, name, specs, out_shape, args, scratch=()):
    return pl.pallas_call(
        kernel,
        in_specs=specs,
        out_specs=[VM] * len(out_shape),
        out_shape=out_shape,
        scratch_shapes=list(scratch),
        compiler_params=params(SUM_VMEM),
        cost_estimate=pl.CostEstimate(flops=FLOPS, bytes_accessed=0, transcendentals=0),
        name=name,
    )(*args)


def plan_kernel(first, place_ref, *refs):
    w_refs, (sums_ref, scale_ref, mark_ref, u_ref, f_ref, d_ref, *refs) = refs[:PARTS], refs[PARTS:]
    plan_ref, mass_ref, up_ref, down_ref, lines_ref = refs
    scale = local_scale(place_ref, sums_ref, lines_ref)
    tiles = tiles_of(w_refs)
    rows = 2 * LANES
    n = plan_ref.shape[0]
    half = n // 2
    for top in range(0, n, rows):
        for at in range(top, top + rows, LANES):
            part = slice(first + at, first + at + LANES)
            line = (first + at) // LANES
            s = down(scale_ref[line : line + 1, :])
            acc = None
            for j, (ref, t) in enumerate(tiles):
                p = ref[part, t : t + LANES] * scale[j]
                acc = p if acc is None else acc + p
                plan_ref[at : at + LANES, j * LANES : (j + 1) * LANES] = (p * s).astype(jnp.bfloat16)
            mass_ref[at // LANES : at // LANES + 1, :] = row_of(acc)
        here = plan_ref[top : top + rows, :]
        far, near, at, v_ref = (up_ref, down_ref, top, d_ref) if top < half else (down_ref, up_ref, top - half, u_ref)
        far[at : at + rows, :] = product(here, f_ref).astype(far.dtype)
        near[half + at : half + at + rows, :] = product(here, v_ref).astype(near.dtype)
    put_tail(up_ref, mass_ref[...])
    put_tail(down_ref, mass_ref[...])


def make_plan(place, w, sums, scale, cuts, first, mark):
    n = w[0].shape[0]
    m, share = cuts[0].shape
    part = jax.ShapeDtypeStruct((n // 2 + TAIL, share), jnp.bfloat16)
    return call(
        lambda *refs: plan_kernel(first, *refs),
        "make_plan",
        [SM] + [VM] * (PARTS + 6),
        [pltpu.VMEM((n // 2, m), jnp.bfloat16), jax.ShapeDtypeStruct((n // 2 // LANES, LANES), jnp.float32), part, part],
        (place, *[held(x) for x in w], sums, scale, mark, *[held(v) for v in cuts[1:]]),
        [pltpu.VMEM(sums.shape[1:], jnp.float32)],
    )


def late_kernel(plan_ref, from_below, from_above, u_ref, d_ref, up_ref, down_ref, mark_ref):
    half = plan_ref.shape[0] // 2
    f32 = jnp.float32
    up = product(plan_ref[:half, :], u_ref) + from_below[:half, :].astype(f32)
    up_ref[:half, :] = up.astype(up_ref.dtype)
    below = product(plan_ref[half:, :], d_ref) + from_above[:half, :].astype(f32)
    down_ref[:half, :] = below.astype(down_ref.dtype)
    up_ref[half:, :] = from_below[2 * half :, :]
    down_ref[half:, :] = from_above[2 * half :, :]
    mark_ref[...] = jnp.zeros_like(mark_ref)


def late_sums(plan, from_below, from_above, cuts):
    n = plan.shape[0]
    share = cuts[0].shape[1]
    out = jax.ShapeDtypeStruct((n // 2 + TAIL, share), jnp.bfloat16)
    mark = jax.ShapeDtypeStruct((8, LANES), jnp.float32)
    return call(
        late_kernel,
        "late_sums",
        [VM] * 5,
        [out, out, mark],
        (held(plan), from_below, from_above, held(cuts[1]), held(cuts[3])),
    )


def own_kernel(index, place_ref, plan_ref, from_below, from_above, v_ref, mark_ref, cents_ref, out_ref, block_ref, sem):
    n, share = out_ref.shape
    half = n // 2
    f32 = jnp.float32
    cols = pl.ds(pl.multiple_of(place_ref[1] * share, share), share)
    copy = pltpu.make_async_copy(cents_ref.at[pl.ds(index * n, n), cols], block_ref, sem)
    copy.start()
    out_ref[:half, :] = product(plan_ref[:half, :], v_ref) + from_above[half : 2 * half, :].astype(f32)
    out_ref[half:, :] = product(plan_ref[half:, :], v_ref) + from_below[half : 2 * half, :].astype(f32)
    copy.wait()


def own_sums(place, plan, from_below, from_above, cuts, mark, centroids, index):
    n, share = plan.shape[0], cuts[0].shape[1]
    return call(
        functools.partial(own_kernel, index),
        "own_sums",
        [SM] + [VM] * 5 + [pl.BlockSpec(memory_space=pltpu.HBM)],
        [pltpu.VMEM((n, share), jnp.float32), pltpu.VMEM((n, share), centroids.dtype)],
        (place, held(plan), from_below, from_above, held(cuts[0]), mark, outside(centroids)),
        [pltpu.SemaphoreType.DMA],
    )


def finish_kernel(index, place_ref, own_ref, scale_ref, m_ref, below, above, up_ref, down_ref, mark_ref, cents_ref, out_ref, mass_ref):
    lines = mass_ref.shape[0]
    scale = scale_ref[index * lines : (index + 1) * lines, :]
    mass_ref[...] = scale * ((m_ref[...] + get_tail(up_ref)) + (get_tail(below) + get_tail(above)))
    n, share = out_ref.shape
    half = n // 2
    f32 = jnp.float32
    for top in range(0, n, LANES):
        part = slice(top, top + LANES)
        line = top // LANES
        late, start = (up_ref, top) if top < half else (down_ref, top - half)
        sums = own_ref[part, :] + late[start : start + LANES, :].astype(f32)
        inverse = down(0.5 / mass_ref[line : line + 1, :])
        for j in range(0, share, LANES):
            value = 0.5 * cents_ref[part, j : j + LANES].astype(f32) + sums[:, j : j + LANES] * inverse
            out_ref[part, j : j + LANES] = value.astype(out_ref.dtype)


def finish(place, own, scale, mass, below, above, up, under, mark, index, whole=None):
    own, block = own
    n, share = own.shape
    lines = n // LANES
    specs = [VM] * 9
    args = [held(own), scale, mass, below, above, up, under, mark, held(block)]
    kernel = functools.partial(finish_kernel, index)
    if whole is not None:
        specs.append(pl.BlockSpec(memory_space=pl.ANY))
        args.append(whole)

        def kernel(*refs):
            finish_kernel(index, *refs[:10], *refs[11:])

    return pl.pallas_call(
        kernel,
        grid_spec=pltpu.PrefetchScalarGridSpec(
            num_scalar_prefetch=1,
            grid=(1,),
            in_specs=specs,
            out_specs=[pl.BlockSpec((n, share), lambda i, place: (index, 0)), VM],
        ),
        out_shape=[
            jax.ShapeDtypeStruct((2 * n, share), jnp.bfloat16),
            jax.ShapeDtypeStruct((lines, LANES), jnp.float32),
        ],
        input_output_aliases={} if whole is None else {10: 0},
        compiler_params=params(SUM_VMEM),
        cost_estimate=pl.CostEstimate(flops=FLOPS, bytes_accessed=0, transcendentals=0),
        name="finish",
    )(place, *args)


def move(x, axis, by):
    n = lax.axis_size(axis)
    return lax.ppermute(x, axis, [(i, (i + by) % n) for i in range(n)])


def spread(x, turn, first):
    if turn == 0:
        return x
    pairs = []
    for i in range(PLACES):
        for j in range(PLACES):
            for core in range(2):
                by_x = (core == 0) == first
                to = ((i + turn) % PLACES, j) if by_x else (i, (j + turn) % PLACES)
                pairs.append(((i * PLACES + j) * 2 + core, (to[0] * PLACES + to[1]) * 2 + core))
    return lax.ppermute(x, CENTS, pairs)


def row_peers(x):
    return x, move(x, "y", 2), move(x, "y", 1), move(x, "y", 3)


def body(vectors, centroids):
    planes = lax.axis_size("y")
    core, x, z, y = [lax.axis_index(name) for name in ("core", "x", "z", "y")]
    first = core == 0
    place = jnp.stack([core, y, jnp.where(first, z, x), jnp.where(first, x, z), jnp.where(first, x, z)])
    place = place.astype(jnp.int32)
    peers = PLACES * PLACES * lax.axis_size("core")
    n, d = centroids.shape
    target = vectors.shape[0] * planes * peers / (n * peers)

    near = in_order(place, [lift(vectors)] + [spread(vectors, turn, True) for turn in range(1, PLACES)])
    size = near.shape[0]
    one, three = spread(near, 1, False), spread(near, 3, False)
    total = size * len(ORDER)
    w0, *old = weigh(place, centroids, (near, move(near, "core", 1)), planes, total, 0)
    mark, one, three = lax.optimization_barrier((old[-1], one, three))
    other = move(one, "core", 1), move(three, "core", 1)
    two = spread(one[: size // 2], 1, False), spread(three[size // 2 :], 3, False)
    w1, *old = weigh(place, centroids, (one, three, *other), planes, total, 2 * size, (*old[:-1], mark))
    mark, *two = lax.optimization_barrier((old[-1], *two))
    other = [move(block, "core", 1) for block in two]
    w2, *cuts, _, colmass = weigh(place, centroids, (*two, *other), planes, total, 6 * size, (*old[:-1], mark))
    w = (w0, w1, w2)

    for step in range(ROUNDS):
        sums, scale = row_pass(target, place, w, row_peers(colmass), peers)
        sums = lax.all_to_all(sums, CENTS, 0, 0, tiled=True)
        if step < ROUNDS - 1:
            colmass = col_pass(place, w, sums)

    mark = jnp.zeros((8, LANES), jnp.float32)
    plan0, mass0, up0, down0 = make_plan(place, w, sums, scale, cuts, 0, mark)
    up0, down0 = move(up0, "y", 1), move(down0, "y", 3)
    plan1, mass1, up1, down1 = make_plan(place, w, sums, scale, cuts, n // 2, mass0)
    up1, down1 = move(up1, "y", 1), move(down1, "y", 3)
    late_up0, late_down0, mark0 = late_sums(plan0, up0, down0, cuts)
    late_up0, late_down0 = move(late_up0, "y", 1), move(late_down0, "y", 3)
    own0 = own_sums(place, plan0, up0, down0, cuts, mark0, centroids, 0)
    late_up1, late_down1, mark1 = late_sums(plan1, up1, down1, cuts)
    late_up1, late_down1 = move(late_up1, "y", 1), move(late_down1, "y", 3)
    own1 = own_sums(place, plan1, up1, down1, cuts, mark1, centroids, 1)
    half, masses0 = finish(place, own0, scale, mass0, up0, down0, late_up0, late_down0, mark1, 0)
    updated, masses1 = finish(
        place, own1, scale, mass1, up1, down1, late_up1, late_down1, mark1, 1, half
    )
    masses = jnp.concatenate([masses0, masses1], axis=0)
    return updated, masses.reshape(n)


def solution(mesh):
    sizes = (mesh.shape["rows"], 4, 4, 2)
    torus = Mesh(mesh.devices.reshape(sizes), ("y",) + CENTS)
    return jax.shard_map(
        body,
        mesh=torus,
        in_specs=(P(("y",) + CENTS, None), P(CENTS, None)),
        out_specs=(P(CENTS, "y"), P(CENTS)),
        check_vma=False,
    )
```

```python
import functools

import jax
import jax.numpy as jnp
from jax import lax
from jax.experimental import pallas as pl
from jax.experimental.pallas import tpu as pltpu
from jax.sharding import Mesh, PartitionSpec as P

ROUNDS = 3
SHARP = 0.75
LOG2E = 1.4426950408889634
CENTS = ("x", "z", "core")
LANES = 128
TAIL = 16
PLACES = 4
PLANES = 4
LINES = 2
SPARE = 8
ORDER = ((True, 0), (False, 0), (True, 1), (True, 3), (False, 1), (False, 3), (True, 2), (False, 2))
PARTS = 3
FLOPS = 3 * 10**10
WEIGH_VMEM = 16 * 1024 * 1024
SUM_VMEM = 10 * 1024 * 1024

VM = pl.BlockSpec(memory_space=pltpu.VMEM)
SM = pl.BlockSpec(memory_space=pltpu.SMEM)


def params(vmem):
    return pltpu.CompilerParams(vmem_limit_bytes=vmem)


def held(x):
    return pltpu.with_memory_space_constraint(x, pltpu.VMEM)


def outside(x):
    return pltpu.with_memory_space_constraint(x, pltpu.HBM)


def row_of(block):
    return jnp.sum(block.T, axis=0, keepdims=True)


def down(row):
    return jnp.broadcast_to(row, (LANES, LANES)).T


def line_of(place_ref, mine, turn):
    core = place_ref[0]
    place, side = (place_ref[2], core) if mine else (place_ref[3], 1 - core)
    return pl.multiple_of((side * PLACES + lax.rem(place + PLACES - turn, PLACES)) * LINES, LINES)


def gather_kernel(place_ref, *refs):
    blocks, out = refs[:-1], refs[-1]
    size = blocks[0].shape[0]
    for turn, block in enumerate(blocks):
        at = lax.rem(place_ref[4] + PLACES - turn, PLACES) * size
        out[pl.ds(pl.multiple_of(at, size), size), :] = block[...]


def in_order(place, blocks):
    size, d = blocks[0].shape
    return pl.pallas_call(
        gather_kernel,
        in_specs=[SM] + [VM] * len(blocks),
        out_specs=VM,
        out_shape=jax.ShapeDtypeStruct((len(blocks) * size, d), blocks[0].dtype),
        compiler_params=params(8 * 1024 * 1024),
        name="in_order",
    )(place, *blocks)


def weigh_kernel(count, at, last, place_ref, cents_ref, *refs):
    blocks = refs[:count]
    olds = 0 if at == 0 else PLANES + 1
    w_ref, *outs = refs[count + olds :]
    cuts, acc_ref = (outs[:-2], outs[-2]) if last else (outs[:-1], outs[-1])
    n = w_ref.shape[0]
    rows = 512
    full = LANES * LINES
    groups = []
    for block in blocks:
        if groups and sum(x.shape[0] for x in groups[-1]) < full:
            groups[-1].append(block)
        else:
            groups.append([block])
    for k in range(0, n, rows):
        acc, left = None if at == 0 else acc_ref[k : k + rows, :], 0
        for group in groups:
            vecs = jnp.concatenate([block[...] for block in group], axis=0)
            cols = vecs.shape[0]
            logits = lax.dot_general(
                cents_ref[k : k + rows, :], vecs, (((1,), (1,)), ((), ())), preferred_element_type=jnp.float32
            )
            w = jnp.exp2(logits * (SHARP * LOG2E))
            w_ref[k : k + rows, left : left + cols] = w
            left += cols
            for j in range(0, cols, LANES):
                acc = w[:, j : j + LANES] if acc is None else acc + w[:, j : j + LANES]
        if not last:
            acc_ref[k : k + rows, :] = acc
        else:
            for g in range(0, rows, LANES):
                line = (k + g) // LANES
                outs[-1][line : line + 1, :] = row_of(acc[g : g + LANES, :])
    for k, cut in enumerate(cuts):
        share, top = cut.shape[1], at
        part = pl.ds(pl.multiple_of(lax.rem(place_ref[1] + k, len(cuts)) * share, share), share)
        for block in blocks:
            cut[top : top + block.shape[0], :] = block[:, part]
            top += block.shape[0]


def weigh(place, cents, blocks, planes, total, at, old=()):
    n, d = cents.shape
    m = sum(block.shape[0] for block in blocks)
    last = at + m == total
    out_shape = [pltpu.VMEM((n, m), jnp.float32)]
    out_shape += [pltpu.VMEM((total, d // planes), cents.dtype) for _ in range(planes)]
    out_shape += [pltpu.VMEM((n, LANES), jnp.float32)]
    if last:
        out_shape += [jax.ShapeDtypeStruct((n // LANES, LANES), jnp.float32)]
    return pl.pallas_call(
        functools.partial(weigh_kernel, len(blocks), at, last),
        in_specs=[SM] + [VM] * (1 + len(blocks) + len(old)),
        out_specs=[VM] * len(out_shape),
        out_shape=out_shape,
        input_output_aliases={2 + len(blocks) + k: 1 + k for k in range(len(old))},
        compiler_params=params(WEIGH_VMEM),
        cost_estimate=pl.CostEstimate(flops=FLOPS, bytes_accessed=0, transcendentals=0),
        name="weigh",
    )(place, held(cents), *[held(x) for x in (*blocks, *old)])


def lift_kernel(x_ref, out_ref):
    out_ref[...] = x_ref[...]


def lift(x):
    return pl.pallas_call(
        lift_kernel,
        in_specs=[VM],
        out_specs=VM,
        out_shape=pltpu.VMEM(x.shape, x.dtype),
        compiler_params=params(8 * 1024 * 1024),
        cost_estimate=pl.CostEstimate(flops=FLOPS, bytes_accessed=0, transcendentals=0),
        name="lift",
    )(outside(x))


def tiles_of(w_refs):
    return [(ref, t) for ref in w_refs for t in range(0, ref.shape[1], LANES)]


def row_kernel(target, place_ref, *refs):
    w_refs, (a_ref, b_ref, c_ref, d_ref, out_ref, scale_ref, lines_ref) = refs[:PARTS], refs[PARTS:]
    scale_ref[...] = target / ((a_ref[...] + b_ref[...]) + (c_ref[...] + d_ref[...]))
    tiles = tiles_of(w_refs)
    accs = [None] * len(tiles)
    for b in range(w_refs[0].shape[0] // LANES):
        part = slice(b * LANES, (b + 1) * LANES)
        s = down(scale_ref[b : b + 1, :])
        for j, (ref, t) in enumerate(tiles):
            p = ref[part, t : t + LANES] * s
            p = jnp.sum(p.reshape(LANES // 8, 8, LANES), axis=0)
            accs[j] = p if b == 0 else accs[j] + p
    for block, (mine, turn) in enumerate(ORDER):
        pair = [jnp.sum(a, axis=0, keepdims=True) for a in accs[block * LINES : (block + 1) * LINES]]
        lines_ref[pl.ds(line_of(place_ref, mine, turn), LINES), :] = jnp.concatenate(pair, axis=0)
    value = lines_ref[: out_ref.shape[1], :].astype(out_ref.dtype)
    for q in range(out_ref.shape[0]):
        out_ref[q] = value


def row_pass(target, place, w, masses, peers):
    n = w[0].shape[0]
    lines = len(ORDER) * LINES
    return pl.pallas_call(
        lambda *refs: row_kernel(target, *refs),
        in_specs=[SM] + [VM] * (PARTS + 4),
        out_specs=[VM, VM],
        out_shape=[
            jax.ShapeDtypeStruct((peers, lines, LANES), jnp.bfloat16),
            jax.ShapeDtypeStruct((n // LANES, LANES), jnp.float32),
        ],
        scratch_shapes=[pltpu.VMEM((lines + SPARE, LANES), jnp.float32)],
        compiler_params=params(8 * 1024 * 1024),
        name="row_pass",
    )(place, *[held(x) for x in w], *masses)


def local_scale(place_ref, sums_ref, lines_ref):
    total = sums_ref[0].astype(jnp.float32)
    for q in range(1, sums_ref.shape[0]):
        total = total + sums_ref[q].astype(jnp.float32)
    lines_ref[: total.shape[0], :] = 1.0 / total
    scale = [lines_ref[pl.ds(line_of(place_ref, mine, turn), LINES), :] for mine, turn in ORDER]
    return [pair[i : i + 1, :] for pair in scale for i in range(LINES)]


def col_kernel(place_ref, *refs):
    w_refs, (sums_ref, out_ref, lines_ref) = refs[:PARTS], refs[PARTS:]
    scale = local_scale(place_ref, sums_ref, lines_ref)
    tiles = tiles_of(w_refs)
    for b in range(w_refs[0].shape[0] // LANES):
        part = slice(b * LANES, (b + 1) * LANES)
        acc = None
        for j, (ref, t) in enumerate(tiles):
            p = ref[part, t : t + LANES] * scale[j]
            acc = p if acc is None else acc + p
        out_ref[b : b + 1, :] = row_of(acc)


def col_pass(place, w, sums):
    n = w[0].shape[0]
    return pl.pallas_call(
        col_kernel,
        in_specs=[SM] + [VM] * (PARTS + 1),
        out_specs=VM,
        out_shape=jax.ShapeDtypeStruct((n // LANES, LANES), jnp.float32),
        scratch_shapes=[pltpu.VMEM((sums.shape[1] + SPARE, LANES), jnp.float32)],
        compiler_params=params(8 * 1024 * 1024),
        name="col_pass",
    )(place, *[held(x) for x in w], sums)


def split(x):
    hi = x.astype(jnp.bfloat16)
    rest = x - hi.astype(jnp.float32)
    mid = rest.astype(jnp.bfloat16)
    return hi, mid, (rest - mid.astype(jnp.float32)).astype(jnp.bfloat16)


def put_tail(ref, x):
    hi, mid, lo = split(x)
    tail = slice(ref.shape[0] - TAIL, ref.shape[0])
    ref[tail, :LANES] = jnp.concatenate([hi, mid], axis=0)
    ref[tail, LANES:] = jnp.concatenate([lo, jnp.zeros_like(lo)], axis=0)


def get_tail(ref):
    f32 = jnp.float32
    tail = slice(ref.shape[0] - TAIL, ref.shape[0])
    first, second = ref[tail, :LANES].astype(f32), ref[tail, LANES:].astype(f32)
    return (first[: TAIL // 2] + first[TAIL // 2 :]) + second[: TAIL // 2]


def product(plan, v_ref):
    return jnp.dot(plan, v_ref[...], preferred_element_type=jnp.float32)


def call(kernel, name, specs, out_shape, args, scratch=()):
    return pl.pallas_call(
        kernel,
        in_specs=specs,
        out_specs=[VM] * len(out_shape),
        out_shape=out_shape,
        scratch_shapes=list(scratch),
        compiler_params=params(SUM_VMEM),
        cost_estimate=pl.CostEstimate(flops=FLOPS, bytes_accessed=0, transcendentals=0),
        name=name,
    )(*args)


def plan_kernel(first, place_ref, *refs):
    w_refs, (sums_ref, scale_ref, mark_ref, u_ref, f_ref, d_ref, *refs) = refs[:PARTS], refs[PARTS:]
    plan_ref, mass_ref, up_ref, down_ref, lines_ref = refs
    scale = local_scale(place_ref, sums_ref, lines_ref)
    tiles = tiles_of(w_refs)
    rows = 2 * LANES
    n = plan_ref.shape[0]
    half = n // 2
    for top in range(0, n, rows):
        for at in range(top, top + rows, LANES):
            part = slice(first + at, first + at + LANES)
            line = (first + at) // LANES
            s = down(scale_ref[line : line + 1, :])
            acc = None
            for j, (ref, t) in enumerate(tiles):
                p = ref[part, t : t + LANES] * scale[j]
                acc = p if acc is None else acc + p
                plan_ref[at : at + LANES, j * LANES : (j + 1) * LANES] = (p * s).astype(jnp.bfloat16)
            mass_ref[at // LANES : at // LANES + 1, :] = row_of(acc)
        here = plan_ref[top : top + rows, :]
        far, near, at, v_ref = (up_ref, down_ref, top, d_ref) if top < half else (down_ref, up_ref, top - half, u_ref)
        far[at : at + rows, :] = product(here, f_ref).astype(far.dtype)
        near[half + at : half + at + rows, :] = product(here, v_ref).astype(near.dtype)
    put_tail(up_ref, mass_ref[...])
    put_tail(down_ref, mass_ref[...])


def make_plan(place, w, sums, scale, cuts, first, mark):
    n = w[0].shape[0]
    m, share = cuts[0].shape
    part = jax.ShapeDtypeStruct((n // 2 + TAIL, share), jnp.bfloat16)
    return call(
        lambda *refs: plan_kernel(first, *refs),
        "make_plan",
        [SM] + [VM] * (PARTS + 6),
        [pltpu.VMEM((n // 2, m), jnp.bfloat16), jax.ShapeDtypeStruct((n // 2 // LANES, LANES), jnp.float32), part, part],
        (place, *[held(x) for x in w], sums, scale, mark, *[held(v) for v in cuts[1:]]),
        [pltpu.VMEM((sums.shape[1] + SPARE, LANES), jnp.float32)],
    )


def late_kernel(plan_ref, from_below, from_above, u_ref, d_ref, up_ref, down_ref, mark_ref):
    half = plan_ref.shape[0] // 2
    f32 = jnp.float32
    up = product(plan_ref[:half, :], u_ref) + from_below[:half, :].astype(f32)
    up_ref[:half, :] = up.astype(up_ref.dtype)
    below = product(plan_ref[half:, :], d_ref) + from_above[:half, :].astype(f32)
    down_ref[:half, :] = below.astype(down_ref.dtype)
    up_ref[half:, :] = from_below[2 * half :, :]
    down_ref[half:, :] = from_above[2 * half :, :]
    mark_ref[...] = jnp.zeros_like(mark_ref)


def late_sums(plan, from_below, from_above, cuts):
    n = plan.shape[0]
    share = cuts[0].shape[1]
    out = jax.ShapeDtypeStruct((n // 2 + TAIL, share), jnp.bfloat16)
    mark = jax.ShapeDtypeStruct((8, LANES), jnp.float32)
    return call(
        late_kernel,
        "late_sums",
        [VM] * 5,
        [out, out, mark],
        (held(plan), from_below, from_above, held(cuts[1]), held(cuts[3])),
    )


def own_kernel(index, place_ref, plan_ref, from_below, from_above, v_ref, mark_ref, cents_ref, out_ref, block_ref, sem):
    n, share = out_ref.shape
    half = n // 2
    f32 = jnp.float32
    cols = pl.ds(pl.multiple_of(place_ref[1] * share, share), share)
    copy = pltpu.make_async_copy(cents_ref.at[pl.ds(index * n, n), cols], block_ref, sem)
    copy.start()
    out_ref[:half, :] = product(plan_ref[:half, :], v_ref) + from_above[half : 2 * half, :].astype(f32)
    out_ref[half:, :] = product(plan_ref[half:, :], v_ref) + from_below[half : 2 * half, :].astype(f32)
    copy.wait()


def own_sums(place, plan, from_below, from_above, cuts, mark, centroids, index):
    n, share = plan.shape[0], cuts[0].shape[1]
    return call(
        functools.partial(own_kernel, index),
        "own_sums",
        [SM] + [VM] * 5 + [pl.BlockSpec(memory_space=pltpu.HBM)],
        [pltpu.VMEM((n, share), jnp.float32), pltpu.VMEM((n, share), centroids.dtype)],
        (place, held(plan), from_below, from_above, held(cuts[0]), mark, outside(centroids)),
        [pltpu.SemaphoreType.DMA],
    )


def finish_kernel(index, place_ref, own_ref, scale_ref, m_ref, below, above, up_ref, down_ref, mark_ref, cents_ref, out_ref, mass_ref):
    lines = mass_ref.shape[0]
    scale = scale_ref[index * lines : (index + 1) * lines, :]
    mass_ref[...] = scale * ((m_ref[...] + get_tail(up_ref)) + (get_tail(below) + get_tail(above)))
    n, share = out_ref.shape
    half = n // 2
    f32 = jnp.float32
    for top in range(0, n, LANES):
        part = slice(top, top + LANES)
        line = top // LANES
        late, start = (up_ref, top) if top < half else (down_ref, top - half)
        sums = own_ref[part, :] + late[start : start + LANES, :].astype(f32)
        inverse = down(0.5 / mass_ref[line : line + 1, :])
        for j in range(0, share, LANES):
            value = 0.5 * cents_ref[part, j : j + LANES].astype(f32) + sums[:, j : j + LANES] * inverse
            out_ref[part, j : j + LANES] = value.astype(out_ref.dtype)


def finish(place, own, scale, mass, below, above, up, under, mark, index, whole=None):
    own, block = own
    n, share = own.shape
    lines = n // LANES
    specs = [VM] * 9
    args = [held(own), scale, mass, below, above, up, under, mark, held(block)]
    kernel = functools.partial(finish_kernel, index)
    if whole is not None:
        specs.append(pl.BlockSpec(memory_space=pl.ANY))
        args.append(whole)

        def kernel(*refs):
            finish_kernel(index, *refs[:10], *refs[11:])

    return pl.pallas_call(
        kernel,
        grid_spec=pltpu.PrefetchScalarGridSpec(
            num_scalar_prefetch=1,
            grid=(1,),
            in_specs=specs,
            out_specs=[pl.BlockSpec((n, share), lambda i, place: (index, 0)), VM],
        ),
        out_shape=[
            jax.ShapeDtypeStruct((2 * n, share), jnp.bfloat16),
            jax.ShapeDtypeStruct((lines, LANES), jnp.float32),
        ],
        input_output_aliases={} if whole is None else {10: 0},
        compiler_params=params(SUM_VMEM),
        cost_estimate=pl.CostEstimate(flops=FLOPS, bytes_accessed=0, transcendentals=0),
        name="finish",
    )(place, *args)


def move(x, axis, by):
    n = lax.axis_size(axis)
    return lax.ppermute(x, axis, [(i, (i + by) % n) for i in range(n)])


def spread(x, turn, first):
    if turn == 0:
        return x
    pairs = []
    for i in range(PLACES):
        for j in range(PLACES):
            for core in range(2):
                by_x = (core == 0) == first
                to = ((i + turn) % PLACES, j) if by_x else (i, (j + turn) % PLACES)
                pairs.append(((i * PLACES + j) * 2 + core, (to[0] * PLACES + to[1]) * 2 + core))
    return lax.ppermute(x, CENTS, pairs)


def row_peers(x):
    return x, move(x, "y", 2), move(x, "y", 1), move(x, "y", 3)


def body(vectors, centroids):
    planes = lax.axis_size("y")
    core, x, z, y = [lax.axis_index(name) for name in ("core", "x", "z", "y")]
    first = core == 0
    place = jnp.stack([core, y, jnp.where(first, z, x), jnp.where(first, x, z), jnp.where(first, x, z)])
    place = place.astype(jnp.int32)
    peers = PLACES * PLACES * lax.axis_size("core")
    n, d = centroids.shape
    target = vectors.shape[0] * planes * peers / (n * peers)

    near = in_order(place, [lift(vectors)] + [spread(vectors, turn, True) for turn in range(1, PLACES)])
    size = near.shape[0]
    one, three = spread(near, 1, False), spread(near, 3, False)
    total = size * len(ORDER)
    w0, *old = weigh(place, centroids, (near, move(near, "core", 1)), planes, total, 0)
    mark, one, three = lax.optimization_barrier((old[-1], one, three))
    other = move(one, "core", 1), move(three, "core", 1)
    two = spread(one[: size // 2], 1, False), spread(three[size // 2 :], 3, False)
    w1, *old = weigh(place, centroids, (one, three, *other), planes, total, 2 * size, (*old[:-1], mark))
    mark, *two = lax.optimization_barrier((old[-1], *two))
    other = [move(block, "core", 1) for block in two]
    w2, *cuts, _, colmass = weigh(place, centroids, (*two, *other), planes, total, 6 * size, (*old[:-1], mark))
    w = (w0, w1, w2)

    for step in range(ROUNDS):
        sums, scale = row_pass(target, place, w, row_peers(colmass), peers)
        sums = lax.all_to_all(sums, CENTS, 0, 0, tiled=True)
        if step < ROUNDS - 1:
            colmass = col_pass(place, w, sums)

    mark = jnp.zeros((8, LANES), jnp.float32)
    plan0, mass0, up0, down0 = make_plan(place, w, sums, scale, cuts, 0, mark)
    up0, down0 = move(up0, "y", 1), move(down0, "y", 3)
    plan1, mass1, up1, down1 = make_plan(place, w, sums, scale, cuts, n // 2, mass0)
    up1, down1 = move(up1, "y", 1), move(down1, "y", 3)
    late_up0, late_down0, mark0 = late_sums(plan0, up0, down0, cuts)
    late_up0, late_down0 = move(late_up0, "y", 1), move(late_down0, "y", 3)
    own0 = own_sums(place, plan0, up0, down0, cuts, mark0, centroids, 0)
    late_up1, late_down1, mark1 = late_sums(plan1, up1, down1, cuts)
    late_up1, late_down1 = move(late_up1, "y", 1), move(late_down1, "y", 3)
    own1 = own_sums(place, plan1, up1, down1, cuts, mark1, centroids, 1)
    half, masses0 = finish(place, own0, scale, mass0, up0, down0, late_up0, late_down0, mark1, 0)
    updated, masses1 = finish(
        place, own1, scale, mass1, up1, down1, late_up1, late_down1, mark1, 1, half
    )
    masses = jnp.concatenate([masses0, masses1], axis=0)
    return updated, masses.reshape(n)


def solution(mesh):
    sizes = (mesh.shape["rows"], 4, 4, 2)
    torus = Mesh(mesh.devices.reshape(sizes), ("y",) + CENTS)
    return jax.shard_map(
        body,
        mesh=torus,
        in_specs=(P(("y",) + CENTS, None), P(CENTS, None)),
        out_specs=(P(CENTS, "y"), P(CENTS)),
        check_vma=False,
    )
```

```python
import functools

import jax
import jax.numpy as jnp
from jax import lax
from jax.experimental import pallas as pl
from jax.experimental.pallas import tpu as pltpu
from jax.sharding import Mesh, PartitionSpec as P

ROUNDS = 3
SHARP = 0.75
LOG2E = 1.4426950408889634
CENTS = ("x", "z", "core")
LANES = 128
TAIL = 16
PLACES = 4
PLANES = 4
LINES = 2
SPARE = 8
ORDER = ((True, 0), (False, 0), (True, 1), (True, 3), (False, 1), (False, 3), (True, 2), (False, 2))
PARTS = 3
FLOPS = 3 * 10**10
WEIGH_VMEM = 16 * 1024 * 1024
SUM_VMEM = 10 * 1024 * 1024

VM = pl.BlockSpec(memory_space=pltpu.VMEM)
SM = pl.BlockSpec(memory_space=pltpu.SMEM)


def params(vmem):
    return pltpu.CompilerParams(vmem_limit_bytes=vmem)


def held(x):
    return pltpu.with_memory_space_constraint(x, pltpu.VMEM)


def outside(x):
    return pltpu.with_memory_space_constraint(x, pltpu.HBM)


def row_of(block):
    return jnp.sum(block.T, axis=0, keepdims=True)


def down(row):
    return jnp.broadcast_to(row, (LANES, LANES)).T


def line_of(place_ref, mine, turn):
    core = place_ref[0]
    place, side = (place_ref[2], core) if mine else (place_ref[3], 1 - core)
    return pl.multiple_of((side * PLACES + lax.rem(place + PLACES - turn, PLACES)) * LINES, LINES)


def gather_kernel(place_ref, *refs):
    blocks, out = refs[:-1], refs[-1]
    size = blocks[0].shape[0]
    for turn, block in enumerate(blocks):
        at = lax.rem(place_ref[4] + PLACES - turn, PLACES) * size
        out[pl.ds(pl.multiple_of(at, size), size), :] = block[...]


def in_order(place, blocks):
    size, d = blocks[0].shape
    return pl.pallas_call(
        gather_kernel,
        in_specs=[SM] + [VM] * len(blocks),
        out_specs=VM,
        out_shape=jax.ShapeDtypeStruct((len(blocks) * size, d), blocks[0].dtype),
        compiler_params=params(8 * 1024 * 1024),
        name="in_order",
    )(place, *blocks)


def weigh_kernel(count, at, last, place_ref, cents_ref, *refs):
    blocks = refs[:count]
    olds = 0 if at == 0 else PLANES + 1
    w_ref, *outs = refs[count + olds :]
    cuts, acc_ref = (outs[:-2], outs[-2]) if last else (outs[:-1], outs[-1])
    n = w_ref.shape[0]
    rows = 512
    full = LANES * LINES
    groups = []
    for block in blocks:
        if groups and sum(x.shape[0] for x in groups[-1]) < full:
            groups[-1].append(block)
        else:
            groups.append([block])
    for k in range(0, n, rows):
        acc, left = None if at == 0 else acc_ref[k : k + rows, :], 0
        for group in groups:
            vecs = jnp.concatenate([block[...] for block in group], axis=0)
            cols = vecs.shape[0]
            logits = lax.dot_general(
                cents_ref[k : k + rows, :], vecs, (((1,), (1,)), ((), ())), preferred_element_type=jnp.float32
            )
            w = jnp.exp2(logits * (SHARP * LOG2E))
            w_ref[k : k + rows, left : left + cols] = w
            left += cols
            for j in range(0, cols, LANES):
                acc = w[:, j : j + LANES] if acc is None else acc + w[:, j : j + LANES]
        if not last:
            acc_ref[k : k + rows, :] = acc
        else:
            for g in range(0, rows, LANES):
                line = (k + g) // LANES
                outs[-1][line : line + 1, :] = row_of(acc[g : g + LANES, :])
    for k, cut in enumerate(cuts):
        share, top = cut.shape[1], at
        part = pl.ds(pl.multiple_of(lax.rem(place_ref[1] + k, len(cuts)) * share, share), share)
        for block in blocks:
            cut[top : top + block.shape[0], :] = block[:, part]
            top += block.shape[0]


def weigh(place, cents, blocks, planes, total, at, old=()):
    n, d = cents.shape
    m = sum(block.shape[0] for block in blocks)
    last = at + m == total
    out_shape = [pltpu.VMEM((n, m), jnp.float32)]
    out_shape += [pltpu.VMEM((total, d // planes), cents.dtype) for _ in range(planes)]
    out_shape += [pltpu.VMEM((n, LANES), jnp.float32)]
    if last:
        out_shape += [jax.ShapeDtypeStruct((n // LANES, LANES), jnp.float32)]
    return pl.pallas_call(
        functools.partial(weigh_kernel, len(blocks), at, last),
        in_specs=[SM] + [VM] * (1 + len(blocks) + len(old)),
        out_specs=[VM] * len(out_shape),
        out_shape=out_shape,
        input_output_aliases={2 + len(blocks) + k: 1 + k for k in range(len(old))},
        compiler_params=params(WEIGH_VMEM),
        cost_estimate=pl.CostEstimate(flops=FLOPS, bytes_accessed=0, transcendentals=0),
        name="weigh",
    )(place, held(cents), *[held(x) for x in (*blocks, *old)])


def lift_kernel(x_ref, out_ref):
    out_ref[...] = x_ref[...]


def lift(x):
    return pl.pallas_call(
        lift_kernel,
        in_specs=[VM],
        out_specs=VM,
        out_shape=pltpu.VMEM(x.shape, x.dtype),
        compiler_params=params(8 * 1024 * 1024),
        cost_estimate=pl.CostEstimate(flops=FLOPS, bytes_accessed=0, transcendentals=0),
        name="lift",
    )(outside(x))


def tiles_of(w_refs):
    return [(ref, t) for ref in w_refs for t in range(0, ref.shape[1], LANES)]


def row_kernel(target, place_ref, *refs):
    w_refs, (a_ref, b_ref, c_ref, d_ref, out_ref, scale_ref, *wide, lines_ref) = refs[:PARTS], refs[PARTS:]
    scale_ref[...] = target / ((a_ref[...] + b_ref[...]) + (c_ref[...] + d_ref[...]))
    tiles = tiles_of(w_refs)
    accs = [None] * len(tiles)
    for b in range(w_refs[0].shape[0] // LANES):
        part = slice(b * LANES, (b + 1) * LANES)
        s = down(scale_ref[b : b + 1, :])
        if wide:
            wide[0][part, :] = s
        for j, (ref, t) in enumerate(tiles):
            p = ref[part, t : t + LANES] * s
            p = jnp.sum(p.reshape(LANES // 8, 8, LANES), axis=0)
            accs[j] = p if b == 0 else accs[j] + p
    for block, (mine, turn) in enumerate(ORDER):
        pair = [jnp.sum(a, axis=0, keepdims=True) for a in accs[block * LINES : (block + 1) * LINES]]
        lines_ref[pl.ds(line_of(place_ref, mine, turn), LINES), :] = jnp.concatenate(pair, axis=0)
    value = lines_ref[: out_ref.shape[1], :].astype(out_ref.dtype)
    for q in range(out_ref.shape[0]):
        out_ref[q] = value


def row_pass(target, place, w, masses, peers, last):
    n = w[0].shape[0]
    wide = [pltpu.VMEM((n, LANES), jnp.float32)] if last else []
    lines = len(ORDER) * LINES
    return pl.pallas_call(
        lambda *refs: row_kernel(target, *refs),
        in_specs=[SM] + [VM] * (PARTS + 4),
        out_specs=[VM] * (2 + len(wide)),
        out_shape=[
            jax.ShapeDtypeStruct((peers, lines, LANES), jnp.bfloat16),
            jax.ShapeDtypeStruct((n // LANES, LANES), jnp.float32),
            *wide,
        ],
        scratch_shapes=[pltpu.VMEM((lines + SPARE, LANES), jnp.float32)],
        compiler_params=params(8 * 1024 * 1024),
        name="row_pass",
    )(place, *[held(x) for x in w], *masses)


def local_scale(place_ref, sums_ref, lines_ref):
    total = sums_ref[0].astype(jnp.float32)
    for q in range(1, sums_ref.shape[0]):
        total = total + sums_ref[q].astype(jnp.float32)
    lines_ref[: total.shape[0], :] = 1.0 / total
    scale = [lines_ref[pl.ds(line_of(place_ref, mine, turn), LINES), :] for mine, turn in ORDER]
    return [pair[i : i + 1, :] for pair in scale for i in range(LINES)]


def col_kernel(place_ref, *refs):
    w_refs, (sums_ref, out_ref, lines_ref) = refs[:PARTS], refs[PARTS:]
    scale = local_scale(place_ref, sums_ref, lines_ref)
    tiles = tiles_of(w_refs)
    for b in range(w_refs[0].shape[0] // LANES):
        part = slice(b * LANES, (b + 1) * LANES)
        acc = None
        for j, (ref, t) in enumerate(tiles):
            p = ref[part, t : t + LANES] * scale[j]
            acc = p if acc is None else acc + p
        out_ref[b : b + 1, :] = row_of(acc)


def col_pass(place, w, sums):
    n = w[0].shape[0]
    return pl.pallas_call(
        col_kernel,
        in_specs=[SM] + [VM] * (PARTS + 1),
        out_specs=VM,
        out_shape=jax.ShapeDtypeStruct((n // LANES, LANES), jnp.float32),
        scratch_shapes=[pltpu.VMEM((sums.shape[1] + SPARE, LANES), jnp.float32)],
        compiler_params=params(8 * 1024 * 1024),
        name="col_pass",
    )(place, *[held(x) for x in w], sums)


def split(x):
    hi = x.astype(jnp.bfloat16)
    rest = x - hi.astype(jnp.float32)
    mid = rest.astype(jnp.bfloat16)
    return hi, mid, (rest - mid.astype(jnp.float32)).astype(jnp.bfloat16)


def put_tail(ref, x):
    hi, mid, lo = split(x)
    tail = slice(ref.shape[0] - TAIL, ref.shape[0])
    ref[tail, :LANES] = jnp.concatenate([hi, mid], axis=0)
    ref[tail, LANES:] = jnp.concatenate([lo, jnp.zeros_like(lo)], axis=0)


def get_tail(ref):
    f32 = jnp.float32
    tail = slice(ref.shape[0] - TAIL, ref.shape[0])
    first, second = ref[tail, :LANES].astype(f32), ref[tail, LANES:].astype(f32)
    return (first[: TAIL // 2] + first[TAIL // 2 :]) + second[: TAIL // 2]


def product(plan, v_ref):
    return jnp.dot(plan, v_ref[...], preferred_element_type=jnp.float32)


def call(kernel, name, specs, out_shape, args, scratch=()):
    return pl.pallas_call(
        kernel,
        in_specs=specs,
        out_specs=[VM] * len(out_shape),
        out_shape=out_shape,
        scratch_shapes=list(scratch),
        compiler_params=params(SUM_VMEM),
        cost_estimate=pl.CostEstimate(flops=FLOPS, bytes_accessed=0, transcendentals=0),
        name=name,
    )(*args)


def plan_kernel(first, place_ref, *refs):
    w_refs, (sums_ref, wide_ref, mark_ref, u_ref, f_ref, d_ref, *refs) = refs[:PARTS], refs[PARTS:]
    plan_ref, mass_ref, up_ref, down_ref, lines_ref = refs
    scale = local_scale(place_ref, sums_ref, lines_ref)
    tiles = tiles_of(w_refs)
    rows = 2 * LANES
    n = plan_ref.shape[0]
    half = n // 2
    for top in range(0, n, rows):
        for at in range(top, top + rows, LANES):
            part = slice(first + at, first + at + LANES)
            line = (first + at) // LANES
            s = wide_ref[part, :]
            acc = None
            for j, (ref, t) in enumerate(tiles):
                p = ref[part, t : t + LANES] * scale[j]
                acc = p if acc is None else acc + p
                plan_ref[at : at + LANES, j * LANES : (j + 1) * LANES] = (p * s).astype(jnp.bfloat16)
            mass_ref[at // LANES : at // LANES + 1, :] = row_of(acc)
        here = plan_ref[top : top + rows, :]
        far, near, at, v_ref = (up_ref, down_ref, top, d_ref) if top < half else (down_ref, up_ref, top - half, u_ref)
        far[at : at + rows, :] = product(here, f_ref).astype(far.dtype)
        near[half + at : half + at + rows, :] = product(here, v_ref).astype(near.dtype)
    put_tail(up_ref, mass_ref[...])
    put_tail(down_ref, mass_ref[...])


def make_plan(place, w, sums, wide, cuts, first, mark):
    n = w[0].shape[0]
    m, share = cuts[0].shape
    part = jax.ShapeDtypeStruct((n // 2 + TAIL, share), jnp.bfloat16)
    return call(
        lambda *refs: plan_kernel(first, *refs),
        "make_plan",
        [SM] + [VM] * (PARTS + 6),
        [pltpu.VMEM((n // 2, m), jnp.bfloat16), jax.ShapeDtypeStruct((n // 2 // LANES, LANES), jnp.float32), part, part],
        (place, *[held(x) for x in w], sums, held(wide), mark, *[held(v) for v in cuts[1:]]),
        [pltpu.VMEM((sums.shape[1] + SPARE, LANES), jnp.float32)],
    )


def late_kernel(plan_ref, from_below, from_above, u_ref, d_ref, up_ref, down_ref, mark_ref):
    half = plan_ref.shape[0] // 2
    f32 = jnp.float32
    up = product(plan_ref[:half, :], u_ref) + from_below[:half, :].astype(f32)
    up_ref[:half, :] = up.astype(up_ref.dtype)
    below = product(plan_ref[half:, :], d_ref) + from_above[:half, :].astype(f32)
    down_ref[:half, :] = below.astype(down_ref.dtype)
    up_ref[half:, :] = from_below[2 * half :, :]
    down_ref[half:, :] = from_above[2 * half :, :]
    mark_ref[...] = jnp.zeros_like(mark_ref)


def late_sums(plan, from_below, from_above, cuts):
    n = plan.shape[0]
    share = cuts[0].shape[1]
    out = jax.ShapeDtypeStruct((n // 2 + TAIL, share), jnp.bfloat16)
    mark = jax.ShapeDtypeStruct((8, LANES), jnp.float32)
    return call(
        late_kernel,
        "late_sums",
        [VM] * 5,
        [out, out, mark],
        (held(plan), from_below, from_above, held(cuts[1]), held(cuts[3])),
    )


def own_kernel(index, place_ref, plan_ref, from_below, from_above, v_ref, mark_ref, cents_ref, out_ref, block_ref, sem):
    n, share = out_ref.shape
    half = n // 2
    f32 = jnp.float32
    cols = pl.ds(pl.multiple_of(place_ref[1] * share, share), share)
    copy = pltpu.make_async_copy(cents_ref.at[pl.ds(index * n, n), cols], block_ref, sem)
    copy.start()
    out_ref[:half, :] = product(plan_ref[:half, :], v_ref) + from_above[half : 2 * half, :].astype(f32)
    out_ref[half:, :] = product(plan_ref[half:, :], v_ref) + from_below[half : 2 * half, :].astype(f32)
    copy.wait()


def own_sums(place, plan, from_below, from_above, cuts, mark, centroids, index):
    n, share = plan.shape[0], cuts[0].shape[1]
    return call(
        functools.partial(own_kernel, index),
        "own_sums",
        [SM] + [VM] * 5 + [pl.BlockSpec(memory_space=pltpu.HBM)],
        [pltpu.VMEM((n, share), jnp.float32), pltpu.VMEM((n, share), centroids.dtype)],
        (place, held(plan), from_below, from_above, held(cuts[0]), mark, outside(centroids)),
        [pltpu.SemaphoreType.DMA],
    )


def finish_kernel(index, place_ref, own_ref, scale_ref, m_ref, below, above, up_ref, down_ref, mark_ref, cents_ref, out_ref, mass_ref):
    lines = mass_ref.shape[0]
    scale = scale_ref[index * lines : (index + 1) * lines, :]
    mass_ref[...] = scale * ((m_ref[...] + get_tail(up_ref)) + (get_tail(below) + get_tail(above)))
    n, share = out_ref.shape
    half = n // 2
    f32 = jnp.float32
    for top in range(0, n, LANES):
        part = slice(top, top + LANES)
        line = top // LANES
        late, start = (up_ref, top) if top < half else (down_ref, top - half)
        sums = own_ref[part, :] + late[start : start + LANES, :].astype(f32)
        inverse = down(0.5 / mass_ref[line : line + 1, :])
        for j in range(0, share, LANES):
            value = 0.5 * cents_ref[part, j : j + LANES].astype(f32) + sums[:, j : j + LANES] * inverse
            out_ref[part, j : j + LANES] = value.astype(out_ref.dtype)


def finish(place, own, scale, mass, below, above, up, under, mark, index, whole=None):
    own, block = own
    n, share = own.shape
    lines = n // LANES
    specs = [VM] * 9
    args = [held(own), scale, mass, below, above, up, under, mark, held(block)]
    kernel = functools.partial(finish_kernel, index)
    if whole is not None:
        specs.append(pl.BlockSpec(memory_space=pl.ANY))
        args.append(whole)

        def kernel(*refs):
            finish_kernel(index, *refs[:10], *refs[11:])

    return pl.pallas_call(
        kernel,
        grid_spec=pltpu.PrefetchScalarGridSpec(
            num_scalar_prefetch=1,
            grid=(1,),
            in_specs=specs,
            out_specs=[pl.BlockSpec((n, share), lambda i, place: (index, 0)), VM],
        ),
        out_shape=[
            jax.ShapeDtypeStruct((2 * n, share), jnp.bfloat16),
            jax.ShapeDtypeStruct((lines, LANES), jnp.float32),
        ],
        input_output_aliases={} if whole is None else {10: 0},
        compiler_params=params(SUM_VMEM),
        cost_estimate=pl.CostEstimate(flops=FLOPS, bytes_accessed=0, transcendentals=0),
        name="finish",
    )(place, *args)


def move(x, axis, by):
    n = lax.axis_size(axis)
    return lax.ppermute(x, axis, [(i, (i + by) % n) for i in range(n)])


def spread(x, turn, first):
    if turn == 0:
        return x
    pairs = []
    for i in range(PLACES):
        for j in range(PLACES):
            for core in range(2):
                by_x = (core == 0) == first
                to = ((i + turn) % PLACES, j) if by_x else (i, (j + turn) % PLACES)
                pairs.append(((i * PLACES + j) * 2 + core, (to[0] * PLACES + to[1]) * 2 + core))
    return lax.ppermute(x, CENTS, pairs)


def row_peers(x):
    return x, move(x, "y", 2), move(x, "y", 1), move(x, "y", 3)


def body(vectors, centroids):
    planes = lax.axis_size("y")
    core, x, z, y = [lax.axis_index(name) for name in ("core", "x", "z", "y")]
    first = core == 0
    place = jnp.stack([core, y, jnp.where(first, z, x), jnp.where(first, x, z), jnp.where(first, x, z)])
    place = place.astype(jnp.int32)
    peers = PLACES * PLACES * lax.axis_size("core")
    n, d = centroids.shape
    target = vectors.shape[0] * planes * peers / (n * peers)

    near = in_order(place, [lift(vectors)] + [spread(vectors, turn, True) for turn in range(1, PLACES)])
    size = near.shape[0]
    one, three = spread(near, 1, False), spread(near, 3, False)
    total = size * len(ORDER)
    w0, *old = weigh(place, centroids, (near, move(near, "core", 1)), planes, total, 0)
    mark, one, three = lax.optimization_barrier((old[-1], one, three))
    other = move(one, "core", 1), move(three, "core", 1)
    two = spread(one[: size // 2], 1, False), spread(three[size // 2 :], 3, False)
    w1, *old = weigh(place, centroids, (one, three, *other), planes, total, 2 * size, (*old[:-1], mark))
    mark, *two = lax.optimization_barrier((old[-1], *two))
    other = [move(block, "core", 1) for block in two]
    w2, *cuts, _, colmass = weigh(place, centroids, (*two, *other), planes, total, 6 * size, (*old[:-1], mark))
    w = (w0, w1, w2)

    for step in range(ROUNDS):
        sums, scale, *wide = row_pass(target, place, w, row_peers(colmass), peers, step == ROUNDS - 1)
        sums = lax.all_to_all(sums, CENTS, 0, 0, tiled=True)
        if step < ROUNDS - 1:
            colmass = col_pass(place, w, sums)

    mark = jnp.zeros((8, LANES), jnp.float32)
    plan0, mass0, up0, down0 = make_plan(place, w, sums, wide[0], cuts, 0, mark)
    up0, down0 = move(up0, "y", 1), move(down0, "y", 3)
    plan1, mass1, up1, down1 = make_plan(place, w, sums, wide[0], cuts, n // 2, mass0)
    up1, down1 = move(up1, "y", 1), move(down1, "y", 3)
    late_up0, late_down0, mark0 = late_sums(plan0, up0, down0, cuts)
    late_up0, late_down0 = move(late_up0, "y", 1), move(late_down0, "y", 3)
    own0 = own_sums(place, plan0, up0, down0, cuts, mark0, centroids, 0)
    late_up1, late_down1, mark1 = late_sums(plan1, up1, down1, cuts)
    late_up1, late_down1 = move(late_up1, "y", 1), move(late_down1, "y", 3)
    own1 = own_sums(place, plan1, up1, down1, cuts, mark1, centroids, 1)
    half, masses0 = finish(place, own0, scale, mass0, up0, down0, late_up0, late_down0, mark1, 0)
    updated, masses1 = finish(
        place, own1, scale, mass1, up1, down1, late_up1, late_down1, mark1, 1, half
    )
    masses = jnp.concatenate([masses0, masses1], axis=0)
    return updated, masses.reshape(n)


def solution(mesh):
    sizes = (mesh.shape["rows"], 4, 4, 2)
    torus = Mesh(mesh.devices.reshape(sizes), ("y",) + CENTS)
    return jax.shard_map(
        body,
        mesh=torus,
        in_specs=(P(("y",) + CENTS, None), P(CENTS, None)),
        out_specs=(P(CENTS, "y"), P(CENTS)),
        check_vma=False,
    )
```

```python
import functools

import jax
import jax.numpy as jnp
from jax import lax
from jax.experimental import pallas as pl
from jax.experimental.pallas import tpu as pltpu
from jax.sharding import Mesh, PartitionSpec as P

ROUNDS = 3
SHARP = 0.75
LOG2E = 1.4426950408889634
CENTS = ("x", "z", "core")
LANES = 128
TAIL = 16
PLACES = 4
PLANES = 4
LINES = 2
SPARE = 8
ORDER = ((True, 0), (False, 0), (True, 1), (True, 3), (False, 1), (False, 3), (True, 2), (False, 2))
PARTS = 3
FLOPS = 3 * 10**10
WEIGH_VMEM = 16 * 1024 * 1024
SUM_VMEM = 10 * 1024 * 1024

VM = pl.BlockSpec(memory_space=pltpu.VMEM)
SM = pl.BlockSpec(memory_space=pltpu.SMEM)


def params(vmem):
    return pltpu.CompilerParams(vmem_limit_bytes=vmem)


def held(x):
    return pltpu.with_memory_space_constraint(x, pltpu.VMEM)


def outside(x):
    return pltpu.with_memory_space_constraint(x, pltpu.HBM)


def row_of(block):
    return jnp.sum(block.T, axis=0, keepdims=True)


def down(row):
    return jnp.broadcast_to(row, (LANES, LANES)).T


def line_of(place_ref, mine, turn):
    core = place_ref[0]
    place, side = (place_ref[2], core) if mine else (place_ref[3], 1 - core)
    return pl.multiple_of((side * PLACES + lax.rem(place + PLACES - turn, PLACES)) * LINES, LINES)


def gather_kernel(place_ref, *refs):
    blocks, out = refs[:-1], refs[-1]
    size = blocks[0].shape[0]
    for turn, block in enumerate(blocks):
        at = lax.rem(place_ref[4] + PLACES - turn, PLACES) * size
        out[pl.ds(pl.multiple_of(at, size), size), :] = block[...]


def in_order(place, blocks):
    size, d = blocks[0].shape
    return pl.pallas_call(
        gather_kernel,
        in_specs=[SM] + [VM] * len(blocks),
        out_specs=VM,
        out_shape=jax.ShapeDtypeStruct((len(blocks) * size, d), blocks[0].dtype),
        compiler_params=params(8 * 1024 * 1024),
        name="in_order",
    )(place, *blocks)


def weigh_kernel(count, at, last, place_ref, cents_ref, *refs):
    blocks = refs[:count]
    olds = 0 if at == 0 else PLANES + 1
    w_ref, *outs = refs[count + olds :]
    cuts, acc_ref = (outs[:-2], outs[-2]) if last else (outs[:-1], outs[-1])
    n = w_ref.shape[0]
    rows = 512
    full = LANES * LINES
    groups = []
    for block in blocks:
        if groups and sum(x.shape[0] for x in groups[-1]) < full:
            groups[-1].append(block)
        else:
            groups.append([block])
    for k in range(0, n, rows):
        acc, left = None if at == 0 else acc_ref[k : k + rows, :], 0
        for group in groups:
            vecs = jnp.concatenate([block[...] for block in group], axis=0)
            cols = vecs.shape[0]
            logits = lax.dot_general(
                cents_ref[k : k + rows, :], vecs, (((1,), (1,)), ((), ())), preferred_element_type=jnp.float32
            )
            w = jnp.exp2(logits * (SHARP * LOG2E))
            w_ref[k : k + rows, left : left + cols] = w
            left += cols
            for j in range(0, cols, LANES):
                acc = w[:, j : j + LANES] if acc is None else acc + w[:, j : j + LANES]
        if not last:
            acc_ref[k : k + rows, :] = acc
        else:
            for g in range(0, rows, LANES):
                line = (k + g) // LANES
                outs[-1][line : line + 1, :] = row_of(acc[g : g + LANES, :])
    for k, cut in enumerate(cuts):
        share, top = cut.shape[1], at
        part = pl.ds(pl.multiple_of(lax.rem(place_ref[1] + k, len(cuts)) * share, share), share)
        for block in blocks:
            cut[top : top + block.shape[0], :] = block[:, part]
            top += block.shape[0]


def weigh(place, cents, blocks, planes, total, at, old=()):
    n, d = cents.shape
    m = sum(block.shape[0] for block in blocks)
    last = at + m == total
    out_shape = [pltpu.VMEM((n, m), jnp.float32)]
    out_shape += [pltpu.VMEM((total, d // planes), cents.dtype) for _ in range(planes)]
    out_shape += [pltpu.VMEM((n, LANES), jnp.float32)]
    if last:
        out_shape += [jax.ShapeDtypeStruct((n // LANES, LANES), jnp.float32)]
    return pl.pallas_call(
        functools.partial(weigh_kernel, len(blocks), at, last),
        in_specs=[SM] + [VM] * (1 + len(blocks) + len(old)),
        out_specs=[VM] * len(out_shape),
        out_shape=out_shape,
        input_output_aliases={2 + len(blocks) + k: 1 + k for k in range(len(old))},
        compiler_params=params(WEIGH_VMEM),
        cost_estimate=pl.CostEstimate(flops=FLOPS, bytes_accessed=0, transcendentals=0),
        name="weigh",
    )(place, held(cents), *[held(x) for x in (*blocks, *old)])


def lift_kernel(x_ref, out_ref):
    out_ref[...] = x_ref[...]


def lift(x):
    return pl.pallas_call(
        lift_kernel,
        in_specs=[VM],
        out_specs=VM,
        out_shape=pltpu.VMEM(x.shape, x.dtype),
        compiler_params=params(8 * 1024 * 1024),
        cost_estimate=pl.CostEstimate(flops=FLOPS, bytes_accessed=0, transcendentals=0),
        name="lift",
    )(outside(x))


def tiles_of(w_refs):
    return [(ref, t) for ref in w_refs for t in range(0, ref.shape[1], LANES)]


def row_kernel(target, place_ref, *refs):
    w_refs, (a_ref, b_ref, c_ref, d_ref, out_ref, scale_ref, *wide, lines_ref) = refs[:PARTS], refs[PARTS:]
    scale_ref[...] = target / ((a_ref[...] + b_ref[...]) + (c_ref[...] + d_ref[...]))
    tiles = tiles_of(w_refs)
    accs = [None] * len(tiles)
    for b in range(w_refs[0].shape[0] // LANES):
        part = slice(b * LANES, (b + 1) * LANES)
        s = down(scale_ref[b : b + 1, :])
        if wide:
            wide[0][part, :] = s
        for j, (ref, t) in enumerate(tiles):
            p = ref[part, t : t + LANES] * s
            p = jnp.sum(p.reshape(LANES // 8, 8, LANES), axis=0)
            accs[j] = p if b == 0 else accs[j] + p
    for block, (mine, turn) in enumerate(ORDER):
        pair = [jnp.sum(a, axis=0, keepdims=True) for a in accs[block * LINES : (block + 1) * LINES]]
        lines_ref[pl.ds(line_of(place_ref, mine, turn), LINES), :] = jnp.concatenate(pair, axis=0)
    value = lines_ref[: out_ref.shape[1], :].astype(out_ref.dtype)
    for q in range(out_ref.shape[0]):
        out_ref[q] = value


def row_pass(target, place, w, masses, peers, last):
    n = w[0].shape[0]
    wide = [pltpu.VMEM((n, LANES), jnp.float32)] if last else []
    lines = len(ORDER) * LINES
    return pl.pallas_call(
        lambda *refs: row_kernel(target, *refs),
        in_specs=[SM] + [VM] * (PARTS + 4),
        out_specs=[VM] * (2 + len(wide)),
        out_shape=[
            jax.ShapeDtypeStruct((peers, lines, LANES), jnp.bfloat16),
            jax.ShapeDtypeStruct((n // LANES, LANES), jnp.float32),
            *wide,
        ],
        scratch_shapes=[pltpu.VMEM((lines + SPARE, LANES), jnp.float32)],
        compiler_params=params(8 * 1024 * 1024),
        name="row_pass",
    )(place, *[held(x) for x in w], *masses)


def local_scale(place_ref, sums_ref, lines_ref):
    total = sums_ref[0].astype(jnp.float32)
    for q in range(1, sums_ref.shape[0]):
        total = total + sums_ref[q].astype(jnp.float32)
    lines_ref[: total.shape[0], :] = 1.0 / total
    scale = [lines_ref[pl.ds(line_of(place_ref, mine, turn), LINES), :] for mine, turn in ORDER]
    return [pair[i : i + 1, :] for pair in scale for i in range(LINES)]


def col_kernel(place_ref, *refs):
    w_refs, (sums_ref, out_ref, lines_ref) = refs[:PARTS], refs[PARTS:]
    scale = local_scale(place_ref, sums_ref, lines_ref)
    tiles = tiles_of(w_refs)
    for b in range(w_refs[0].shape[0] // LANES):
        part = slice(b * LANES, (b + 1) * LANES)
        acc = None
        for j, (ref, t) in enumerate(tiles):
            p = ref[part, t : t + LANES] * scale[j]
            acc = p if acc is None else acc + p
        out_ref[b : b + 1, :] = row_of(acc)


def col_pass(place, w, sums):
    n = w[0].shape[0]
    return pl.pallas_call(
        col_kernel,
        in_specs=[SM] + [VM] * (PARTS + 1),
        out_specs=VM,
        out_shape=jax.ShapeDtypeStruct((n // LANES, LANES), jnp.float32),
        scratch_shapes=[pltpu.VMEM((sums.shape[1] + SPARE, LANES), jnp.float32)],
        compiler_params=params(8 * 1024 * 1024),
        name="col_pass",
    )(place, *[held(x) for x in w], sums)


def split(x):
    hi = x.astype(jnp.bfloat16)
    rest = x - hi.astype(jnp.float32)
    mid = rest.astype(jnp.bfloat16)
    return hi, mid, (rest - mid.astype(jnp.float32)).astype(jnp.bfloat16)


def put_tail(ref, x):
    hi, mid, lo = split(x)
    tail = slice(ref.shape[0] - TAIL, ref.shape[0])
    ref[tail, :LANES] = jnp.concatenate([hi, mid], axis=0)
    ref[tail, LANES:] = jnp.concatenate([lo, jnp.zeros_like(lo)], axis=0)


def get_tail(ref):
    f32 = jnp.float32
    tail = slice(ref.shape[0] - TAIL, ref.shape[0])
    first, second = ref[tail, :LANES].astype(f32), ref[tail, LANES:].astype(f32)
    return (first[: TAIL // 2] + first[TAIL // 2 :]) + second[: TAIL // 2]


def product(plan, v_ref):
    return jnp.dot(plan, v_ref[...], preferred_element_type=jnp.float32)


def call(kernel, name, specs, out_shape, args, scratch=()):
    return pl.pallas_call(
        kernel,
        in_specs=specs,
        out_specs=[VM] * len(out_shape),
        out_shape=out_shape,
        scratch_shapes=list(scratch),
        compiler_params=params(SUM_VMEM),
        cost_estimate=pl.CostEstimate(flops=FLOPS, bytes_accessed=0, transcendentals=0),
        name=name,
    )(*args)


def plan_kernel(first, place_ref, *refs):
    w_refs, (sums_ref, wide_ref, mark_ref, u_ref, f_ref, d_ref, *refs) = refs[:PARTS], refs[PARTS:]
    plan_ref, mass_ref, up_ref, down_ref, lines_ref = refs
    scale = local_scale(place_ref, sums_ref, lines_ref)
    tiles = tiles_of(w_refs)
    rows = 4 * LANES
    n = plan_ref.shape[0]
    half = n // 2
    for top in range(0, n, rows):
        for at in range(top, top + rows, LANES):
            part = slice(first + at, first + at + LANES)
            line = (first + at) // LANES
            s = wide_ref[part, :]
            acc = None
            for j, (ref, t) in enumerate(tiles):
                p = ref[part, t : t + LANES] * scale[j]
                acc = p if acc is None else acc + p
                plan_ref[at : at + LANES, j * LANES : (j + 1) * LANES] = (p * s).astype(jnp.bfloat16)
            mass_ref[at // LANES : at // LANES + 1, :] = row_of(acc)
        here = plan_ref[top : top + rows, :]
        far, near, at, v_ref = (up_ref, down_ref, top, d_ref) if top < half else (down_ref, up_ref, top - half, u_ref)
        far[at : at + rows, :] = product(here, f_ref).astype(far.dtype)
        near[half + at : half + at + rows, :] = product(here, v_ref).astype(near.dtype)
    put_tail(up_ref, mass_ref[...])
    put_tail(down_ref, mass_ref[...])


def make_plan(place, w, sums, wide, cuts, first, mark):
    n = w[0].shape[0]
    m, share = cuts[0].shape
    part = jax.ShapeDtypeStruct((n // 2 + TAIL, share), jnp.bfloat16)
    return call(
        lambda *refs: plan_kernel(first, *refs),
        "make_plan",
        [SM] + [VM] * (PARTS + 6),
        [pltpu.VMEM((n // 2, m), jnp.bfloat16), jax.ShapeDtypeStruct((n // 2 // LANES, LANES), jnp.float32), part, part],
        (place, *[held(x) for x in w], sums, held(wide), mark, *[held(v) for v in cuts[1:]]),
        [pltpu.VMEM((sums.shape[1] + SPARE, LANES), jnp.float32)],
    )


def late_kernel(plan_ref, from_below, from_above, u_ref, d_ref, up_ref, down_ref, mark_ref):
    half = plan_ref.shape[0] // 2
    f32 = jnp.float32
    up = product(plan_ref[:half, :], u_ref) + from_below[:half, :].astype(f32)
    up_ref[:half, :] = up.astype(up_ref.dtype)
    below = product(plan_ref[half:, :], d_ref) + from_above[:half, :].astype(f32)
    down_ref[:half, :] = below.astype(down_ref.dtype)
    up_ref[half:, :] = from_below[2 * half :, :]
    down_ref[half:, :] = from_above[2 * half :, :]
    mark_ref[...] = jnp.zeros_like(mark_ref)


def late_sums(plan, from_below, from_above, cuts):
    n = plan.shape[0]
    share = cuts[0].shape[1]
    out = jax.ShapeDtypeStruct((n // 2 + TAIL, share), jnp.bfloat16)
    mark = jax.ShapeDtypeStruct((8, LANES), jnp.float32)
    return call(
        late_kernel,
        "late_sums",
        [VM] * 5,
        [out, out, mark],
        (held(plan), from_below, from_above, held(cuts[1]), held(cuts[3])),
    )


def own_kernel(index, place_ref, plan_ref, from_below, from_above, v_ref, mark_ref, cents_ref, out_ref, block_ref, sem):
    n, share = out_ref.shape
    half = n // 2
    f32 = jnp.float32
    cols = pl.ds(pl.multiple_of(place_ref[1] * share, share), share)
    copy = pltpu.make_async_copy(cents_ref.at[pl.ds(index * n, n), cols], block_ref, sem)
    copy.start()
    out_ref[:half, :] = product(plan_ref[:half, :], v_ref) + from_above[half : 2 * half, :].astype(f32)
    out_ref[half:, :] = product(plan_ref[half:, :], v_ref) + from_below[half : 2 * half, :].astype(f32)
    copy.wait()


def own_sums(place, plan, from_below, from_above, cuts, mark, centroids, index):
    n, share = plan.shape[0], cuts[0].shape[1]
    return call(
        functools.partial(own_kernel, index),
        "own_sums",
        [SM] + [VM] * 5 + [pl.BlockSpec(memory_space=pltpu.HBM)],
        [pltpu.VMEM((n, share), jnp.float32), pltpu.VMEM((n, share), centroids.dtype)],
        (place, held(plan), from_below, from_above, held(cuts[0]), mark, outside(centroids)),
        [pltpu.SemaphoreType.DMA],
    )


def finish_kernel(index, place_ref, own_ref, scale_ref, m_ref, below, above, up_ref, down_ref, mark_ref, cents_ref, out_ref, mass_ref):
    lines = mass_ref.shape[0]
    scale = scale_ref[index * lines : (index + 1) * lines, :]
    mass_ref[...] = scale * ((m_ref[...] + get_tail(up_ref)) + (get_tail(below) + get_tail(above)))
    n, share = out_ref.shape
    half = n // 2
    f32 = jnp.float32
    for top in range(0, n, LANES):
        part = slice(top, top + LANES)
        line = top // LANES
        late, start = (up_ref, top) if top < half else (down_ref, top - half)
        sums = own_ref[part, :] + late[start : start + LANES, :].astype(f32)
        inverse = down(0.5 / mass_ref[line : line + 1, :])
        for j in range(0, share, LANES):
            value = 0.5 * cents_ref[part, j : j + LANES].astype(f32) + sums[:, j : j + LANES] * inverse
            out_ref[part, j : j + LANES] = value.astype(out_ref.dtype)


def finish(place, own, scale, mass, below, above, up, under, mark, index, whole=None):
    own, block = own
    n, share = own.shape
    lines = n // LANES
    specs = [VM] * 9
    args = [held(own), scale, mass, below, above, up, under, mark, held(block)]
    kernel = functools.partial(finish_kernel, index)
    if whole is not None:
        specs.append(pl.BlockSpec(memory_space=pl.ANY))
        args.append(whole)

        def kernel(*refs):
            finish_kernel(index, *refs[:10], *refs[11:])

    return pl.pallas_call(
        kernel,
        grid_spec=pltpu.PrefetchScalarGridSpec(
            num_scalar_prefetch=1,
            grid=(1,),
            in_specs=specs,
            out_specs=[pl.BlockSpec((n, share), lambda i, place: (index, 0)), VM],
        ),
        out_shape=[
            jax.ShapeDtypeStruct((2 * n, share), jnp.bfloat16),
            jax.ShapeDtypeStruct((lines, LANES), jnp.float32),
        ],
        input_output_aliases={} if whole is None else {10: 0},
        compiler_params=params(SUM_VMEM),
        cost_estimate=pl.CostEstimate(flops=FLOPS, bytes_accessed=0, transcendentals=0),
        name="finish",
    )(place, *args)


def move(x, axis, by):
    n = lax.axis_size(axis)
    return lax.ppermute(x, axis, [(i, (i + by) % n) for i in range(n)])


def spread(x, turn, first):
    if turn == 0:
        return x
    pairs = []
    for i in range(PLACES):
        for j in range(PLACES):
            for core in range(2):
                by_x = (core == 0) == first
                to = ((i + turn) % PLACES, j) if by_x else (i, (j + turn) % PLACES)
                pairs.append(((i * PLACES + j) * 2 + core, (to[0] * PLACES + to[1]) * 2 + core))
    return lax.ppermute(x, CENTS, pairs)


def row_peers(x):
    return x, move(x, "y", 2), move(x, "y", 1), move(x, "y", 3)


def body(vectors, centroids):
    planes = lax.axis_size("y")
    core, x, z, y = [lax.axis_index(name) for name in ("core", "x", "z", "y")]
    first = core == 0
    place = jnp.stack([core, y, jnp.where(first, z, x), jnp.where(first, x, z), jnp.where(first, x, z)])
    place = place.astype(jnp.int32)
    peers = PLACES * PLACES * lax.axis_size("core")
    n, d = centroids.shape
    target = vectors.shape[0] * planes * peers / (n * peers)

    near = in_order(place, [lift(vectors)] + [spread(vectors, turn, True) for turn in range(1, PLACES)])
    size = near.shape[0]
    one, three = spread(near, 1, False), spread(near, 3, False)
    total = size * len(ORDER)
    w0, *old = weigh(place, centroids, (near, move(near, "core", 1)), planes, total, 0)
    mark, one, three = lax.optimization_barrier((old[-1], one, three))
    other = move(one, "core", 1), move(three, "core", 1)
    two = spread(one[: size // 2], 1, False), spread(three[size // 2 :], 3, False)
    w1, *old = weigh(place, centroids, (one, three, *other), planes, total, 2 * size, (*old[:-1], mark))
    mark, *two = lax.optimization_barrier((old[-1], *two))
    other = [move(block, "core", 1) for block in two]
    w2, *cuts, _, colmass = weigh(place, centroids, (*two, *other), planes, total, 6 * size, (*old[:-1], mark))
    w = (w0, w1, w2)

    for step in range(ROUNDS):
        sums, scale, *wide = row_pass(target, place, w, row_peers(colmass), peers, step == ROUNDS - 1)
        sums = lax.all_to_all(sums, CENTS, 0, 0, tiled=True)
        if step < ROUNDS - 1:
            colmass = col_pass(place, w, sums)

    mark = jnp.zeros((8, LANES), jnp.float32)
    plan0, mass0, up0, down0 = make_plan(place, w, sums, wide[0], cuts, 0, mark)
    up0, down0 = move(up0, "y", 1), move(down0, "y", 3)
    plan1, mass1, up1, down1 = make_plan(place, w, sums, wide[0], cuts, n // 2, mass0)
    up1, down1 = move(up1, "y", 1), move(down1, "y", 3)
    late_up0, late_down0, mark0 = late_sums(plan0, up0, down0, cuts)
    late_up0, late_down0 = move(late_up0, "y", 1), move(late_down0, "y", 3)
    own0 = own_sums(place, plan0, up0, down0, cuts, mark0, centroids, 0)
    late_up1, late_down1, mark1 = late_sums(plan1, up1, down1, cuts)
    late_up1, late_down1 = move(late_up1, "y", 1), move(late_down1, "y", 3)
    own1 = own_sums(place, plan1, up1, down1, cuts, mark1, centroids, 1)
    half, masses0 = finish(place, own0, scale, mass0, up0, down0, late_up0, late_down0, mark1, 0)
    updated, masses1 = finish(
        place, own1, scale, mass1, up1, down1, late_up1, late_down1, mark1, 1, half
    )
    masses = jnp.concatenate([masses0, masses1], axis=0)
    return updated, masses.reshape(n)


def solution(mesh):
    sizes = (mesh.shape["rows"], 4, 4, 2)
    torus = Mesh(mesh.devices.reshape(sizes), ("y",) + CENTS)
    return jax.shard_map(
        body,
        mesh=torus,
        in_specs=(P(("y",) + CENTS, None), P(CENTS, None)),
        out_specs=(P(CENTS, "y"), P(CENTS)),
        check_vma=False,
    )
```
